128 devices in a mesh: rep: 16 (over y, z_lo, core), fsdp: 8 (over z_hi, x).
Axes of the slice: x: 4, y: 4, z: 4 (z_hi: 2, z_lo: 2; z = z_hi * 2 + z_lo), core: 2. Of those that a mesh axis runs over, the one named last changes fastest.
Arguments:
- tokens: bfloat16 [22528, 960], P(('rep', 'fsdp')), may hold values from -6 to 6
- seq_lengths: int32 [16, 3], P('rep'), may hold values from 1 to 1406, as said below
- attn_gain: bfloat16 [2, 960], P(None, 'fsdp'), may hold values from 0.5 to 1.5
- query_weight: bfloat16 [2, 960, 960], P(None, 'fsdp'), may hold values from -0.1875 to 0.1875
- key_projection: bfloat16 [2, 960, 320], P(None, 'fsdp'), may hold values from -0.1875 to 0.1875
- value_projection: bfloat16 [2, 960, 320], P(None, 'fsdp'), may hold values from -0.1875 to 0.1875
- out_weight: bfloat16 [2, 960, 960], P(None, 'fsdp'), may hold values from -0.75 to 0.75
- mlp_gain: bfloat16 [2, 960], P(None, 'fsdp'), may hold values from 0.5 to 1.5
- gate_weight: bfloat16 [2, 960, 2560], P(None, 'fsdp'), may hold values from -0.1875 to 0.1875
- up_weight: bfloat16 [2, 960, 2560], P(None, 'fsdp'), may hold values from -0.1875 to 0.1875
- down_weight: bfloat16 [2, 2560, 960], P(None, 'fsdp'), may hold values from -0.125 to 0.125
- cotangent: bfloat16 [22528, 960], P(('rep', 'fsdp')), may hold values from -6 to 6
Outputs:
- output: bfloat16 [22528, 960], P(('rep', 'fsdp'))
- grad_tokens: float32 [22528, 960], P(('rep', 'fsdp'))
- grad_attn_gain: float32 [2, 960], P(None, 'fsdp')
- grad_query_weight: float32 [2, 960, 960], P(None, 'fsdp')
- grad_key_weight: float32 [2, 960, 320], P(None, 'fsdp')
- grad_value_weight: float32 [2, 960, 320], P(None, 'fsdp')
- grad_out_weight: float32 [2, 960, 960], P(None, 'fsdp')
- grad_mlp_gain: float32 [2, 960], P(None, 'fsdp')
- grad_gate_weight: float32 [2, 960, 2560], P(None, 'fsdp')
- grad_up_weight: float32 [2, 960, 2560], P(None, 'fsdp')
- grad_down_weight: float32 [2, 2560, 960], P(None, 'fsdp')
The draws below stay inside these ranges and needn't reach their ends.
Inputs may be any that keep to these rules, and one draw needn't show every extreme that they name: `seq_lengths`: row r gives the lengths of the 3 sequences of pack r in order; they sum to 1408, and the first and the last are under 176.
All inputs are finite; a program needn't handle non-finite values.
Results may differ from the reference program's by a relative error of at most 0.03.
Values may be sent and summed in bfloat16 or wider, within the bound.
No kernel may reach another device: no remote copies, remote signals or barrier semaphores. Data moves between devices by JAX's collectives and lax.ppermute only.
A program may use at most 256 MiB of HBM per device.

```python
import jax
import jax.numpy as jnp
from jax import lax

MODEL_WIDTH = 960
QUERY_HEADS = 15
KEY_VALUE_HEADS = 5
HEAD_SIZE = 64
FF = 2560
DECODER_LAYERS = 2
TOK_DEV = 176
PACK_TOKENS = 1408
TOKENS = 22528
N_REP = 16
N_FSDP = 8


def draw_seq_lengths(key, part):
    key = jax.random.fold_in(key, 7)
    first_key, last_key, pick_key = jax.random.split(key, 3)
    first_len = jax.random.randint(first_key, (N_REP,), 1, TOK_DEV)
    last_len = jax.random.randint(last_key, (N_REP,), 1, TOK_DEV)
    picked = jax.random.randint(pick_key, (), 0, N_REP)
    chosen_row = jnp.arange(N_REP, dtype=jnp.int32) == picked
    first_len = jnp.where(chosen_row, 1, first_len)
    last_len = jnp.where(chosen_row, 1, last_len)
    middle_len = TOK_DEV * N_FSDP - first_len - last_len
    return jnp.stack([first_len, middle_len, last_len], axis=1).astype(jnp.int32)


def block_levels(key, extent, pieces, low, high):
    level = 1.0
    for position, shards_of in pieces:
        heights = jax.random.uniform(jax.random.fold_in(jax.random.fold_in(key, 6), position), (shards_of,), jnp.float32, low / len(pieces), high / len(pieces))
        level = level * jnp.repeat(jnp.exp(heights), extent[position] // shards_of).reshape((-1,) + (1,) * (len(extent) - 1 - position))
    return level


def scatter_about(own_key, extent, spread, reach, cuts=(), held_as=jnp.bfloat16):
    level = block_levels(own_key, extent, cuts, -0.22, 0.18) if cuts else 1.0
    entries = jax.random.normal(own_key, extent, jnp.float32) * spread * level
    return jnp.minimum(jnp.maximum(entries, -reach), reach).astype(held_as)


def setup_inputs(seed: int = 0) -> dict:
    keys = jax.random.split(jax.random.key(seed), 13)
    return {
        "tokens": scatter_about(keys[0], (TOKENS, MODEL_WIDTH), 1.0, 6.0, ((0, 128),)),
        "seq_lengths": draw_seq_lengths(jax.random.fold_in(keys[12], 71), 0),
        "attn_gain": jnp.clip(1.0 + 0.1 * jax.random.normal(keys[2], (DECODER_LAYERS, MODEL_WIDTH), jnp.float32), 0.5, 1.5).astype(jnp.bfloat16),
        "query_weight": scatter_about(keys[3], (DECODER_LAYERS, MODEL_WIDTH, QUERY_HEADS * HEAD_SIZE), MODEL_WIDTH ** -0.5, 0.1875, ((1, 8),)),
        "key_projection": scatter_about(keys[4], (DECODER_LAYERS, MODEL_WIDTH, KEY_VALUE_HEADS * HEAD_SIZE), MODEL_WIDTH ** -0.5, 0.1875, ((1, 8),)),
        "value_projection": scatter_about(keys[5], (DECODER_LAYERS, MODEL_WIDTH, KEY_VALUE_HEADS * HEAD_SIZE), MODEL_WIDTH ** -0.5, 0.1875, ((1, 8),)),
        "out_weight": scatter_about(keys[6], (DECODER_LAYERS, QUERY_HEADS * HEAD_SIZE, MODEL_WIDTH), (QUERY_HEADS * HEAD_SIZE // 16) ** -0.5, 0.75, ((1, 8),)),
        "mlp_gain": jnp.clip(1.0 + 0.1 * jax.random.normal(keys[7], (DECODER_LAYERS, MODEL_WIDTH), jnp.float32), 0.5, 1.5).astype(jnp.bfloat16),
        "gate_weight": scatter_about(keys[8], (DECODER_LAYERS, MODEL_WIDTH, FF), MODEL_WIDTH ** -0.5, 0.1875, ((1, 8),)),
        "up_weight": scatter_about(keys[9], (DECODER_LAYERS, MODEL_WIDTH, FF), MODEL_WIDTH ** -0.5, 0.1875, ((1, 8),)),
        "down_weight": scatter_about(keys[10], (DECODER_LAYERS, FF, MODEL_WIDTH), FF ** -0.5, 0.125, ((1, 8),)),
        "cotangent": scatter_about(keys[11], (TOKENS, MODEL_WIDTH), 1.0, 6.0, ((0, 128),)),
    }


epsilon_norm = 1e-05
rope_base = 100000.0
masked_score = -1e+30
highest_precision = lax.Precision.HIGHEST

@jax.custom_vjp
def reduced_precision(v):
    return lax.optimization_barrier(v.astype(jnp.bfloat16)).astype(jnp.float32)

@jax.custom_vjp
def reduced_backward(v):
    return v

def low_keep(v):
    return (reduced_precision(v), None)

def low_pass(kept, grad):
    return (grad,)

def back_keep(v):
    return (v, None)

def back_low(kept, grad):
    return (reduced_precision(grad),)
reduced_precision.defvjp(low_keep, low_pass)
reduced_backward.defvjp(back_keep, back_low)

def rms_scale(stream, gain):
    return stream * lax.rsqrt(lax.optimization_barrier(jnp.mean(stream * stream, axis=-1, keepdims=True)) + epsilon_norm) * gain

def rotary(head_values, cosine_table, sine_values):
    half_dim = head_values.shape[-1] // 2
    turned = jnp.concatenate([-head_values[..., half_dim:], head_values[..., :half_dim]], axis=-1)
    return head_values * cosine_table[:, None, :] + turned * sine_values[:, None, :]

def rope_tables(positions):
    frequency = rope_base ** (-(jnp.arange(HEAD_SIZE // 2, dtype=jnp.float32) * 2.0) / HEAD_SIZE)
    angles = positions[:, None] * frequency[None, :]
    angles = jnp.concatenate([angles, angles], axis=1)
    return (jnp.cos(angles), jnp.sin(angles))

def segment_layout(lengths, group_pos):
    seq_ends = jnp.cumsum(lengths).astype(jnp.int32)
    seq_starts = (seq_ends - lengths).astype(jnp.int32)
    segment = lax.optimization_barrier(jnp.sum((group_pos[:, None] >= seq_ends[None, :-1]).astype(jnp.int32), axis=1)).astype(jnp.int32)
    chosen = (segment[:, None] == jnp.arange(lengths.shape[0], dtype=jnp.int32)[None, :]).astype(jnp.int32)
    offsets = group_pos - lax.optimization_barrier(jnp.sum(chosen * seq_starts[None, :], axis=1)).astype(jnp.int32)
    return (segment, offsets.astype(jnp.float32))

def attend_pack(arguments):
    query_rows, heads_of_keys, value_rows, segment = arguments
    group_pos = jnp.arange(query_rows.shape[0], dtype=jnp.int32)
    scores = jnp.einsum('qhgd,khd->hgqk', query_rows, heads_of_keys, precision=highest_precision) * HEAD_SIZE ** (-0.5)
    scores = reduced_backward(scores)
    allowed = (segment[:, None] == segment[None, :]) & (group_pos[None, :] <= group_pos[:, None])
    scores = jnp.where(allowed[None, None], scores, masked_score)
    soft_weights = reduced_precision(jax.nn.softmax(scores, axis=-1))
    return jnp.einsum('hgqk,khd->qhgd', soft_weights, value_rows, precision=highest_precision)

def residual_block(stream, cosine_table, sine_values, segment_ids, parameters):
    attn_gain, query_weight, key_projection, value_projection, out_weight, mlp_gain, gate_weight, up_weight, down_weight = parameters
    count_of_rows = stream.shape[0]
    token_packs = count_of_rows // PACK_TOKENS
    normalized_input = reduced_precision(rms_scale(stream, attn_gain))
    query_rows = reduced_backward(jnp.dot(normalized_input, query_weight, precision=highest_precision)).reshape(count_of_rows, QUERY_HEADS, HEAD_SIZE)
    query_rows = reduced_precision(rotary(query_rows, cosine_table, sine_values))
    heads_of_keys = reduced_backward(jnp.dot(normalized_input, key_projection, precision=highest_precision)).reshape(count_of_rows, KEY_VALUE_HEADS, HEAD_SIZE)
    heads_of_keys = reduced_precision(rotary(heads_of_keys, cosine_table, sine_values))
    value_rows = reduced_precision(reduced_backward(jnp.dot(normalized_input, value_projection, precision=highest_precision))).reshape(count_of_rows, KEY_VALUE_HEADS, HEAD_SIZE)
    combined_heads = lax.map(jax.checkpoint(attend_pack), (query_rows.reshape(token_packs, PACK_TOKENS, KEY_VALUE_HEADS, QUERY_HEADS // KEY_VALUE_HEADS, HEAD_SIZE), heads_of_keys.reshape(token_packs, PACK_TOKENS, KEY_VALUE_HEADS, HEAD_SIZE), value_rows.reshape(token_packs, PACK_TOKENS, KEY_VALUE_HEADS, HEAD_SIZE), segment_ids))
    combined_heads = reduced_backward(reduced_precision(combined_heads.reshape(count_of_rows, QUERY_HEADS * HEAD_SIZE)))
    stream = stream + reduced_backward(jnp.dot(combined_heads, out_weight, precision=highest_precision))
    normalized_input = reduced_precision(rms_scale(stream, mlp_gain))
    gate_value = reduced_backward(jnp.dot(normalized_input, gate_weight, precision=highest_precision))
    up_value = reduced_backward(jnp.dot(normalized_input, up_weight, precision=highest_precision))
    hidden = reduced_precision(jax.nn.silu(gate_value) * up_value)
    return stream + reduced_backward(jnp.dot(hidden, down_weight, precision=highest_precision))

def reference(tokens, seq_lengths, attn_gain, query_weight, key_projection, value_projection, out_weight, mlp_gain, gate_weight, up_weight, down_weight, cotangent):
    group_pos = jnp.arange(PACK_TOKENS, dtype=jnp.int32)
    segment_ids, offsets = jax.vmap(lambda lengths: segment_layout(lengths, group_pos))(seq_lengths)
    cosine_table, sine_values = rope_tables(offsets.reshape(-1))
    parameters = tuple((argument_array.astype(jnp.float32) for argument_array in (attn_gain, query_weight, key_projection, value_projection, out_weight, mlp_gain, gate_weight, up_weight, down_weight)))

    def forward_pass(stream, gains_attn, queries_w, keys_w, values_w, outs_w, gains_mlp, gates_w, ups_w, downs_w):
        for layer_index in range(DECODER_LAYERS):
            stream = residual_block(stream, cosine_table, sine_values, segment_ids, (gains_attn[layer_index], queries_w[layer_index], keys_w[layer_index], values_w[layer_index], outs_w[layer_index], gains_mlp[layer_index], gates_w[layer_index], ups_w[layer_index], downs_w[layer_index]))
        return stream
    result, backward = jax.vjp(forward_pass, tokens.astype(jnp.float32), *parameters)
    grads = backward(cotangent.astype(jnp.float32))
    return (result.astype(jnp.bfloat16), grads[0], grads[1], grads[2], grads[3], grads[4], grads[5], grads[6], grads[7], grads[8], grads[9])
```

```python
import functools

import jax
import jax.numpy as jnp
from jax import lax
from jax.experimental import pallas as pl
from jax.experimental.pallas import tpu as pltpu
from jax.sharding import PartitionSpec as P

QUERY_HEADS = 15
KEY_VALUE_HEADS = 5
GROUP = QUERY_HEADS // KEY_VALUE_HEADS
HEAD = 64
DECODER_LAYERS = 2
X_SIZE = 4

epsilon_norm = 1e-05
rope_base = 100000.0
masked_score = -1e30

f32 = jnp.float32
bf16 = jnp.bfloat16

NT = (((1,), (1,)), ((), ()))


def swap(array, axis, mask):
    count = lax.axis_size(axis)
    return lax.ppermute(array, axis, [(i, i ^ mask) for i in range(count)])


def swap_core(array):
    return swap(array, "rep", 1)


def gather_pack(rows):
    pair = jnp.stack([rows, swap(rows, "fsdp", 4)])
    parts = [pair] + [swap(pair, "fsdp", m) for m in range(1, X_SIZE)]
    return jnp.concatenate(parts, axis=0).reshape(-1, rows.shape[-1])


BLOCK_ORDER = (0, 4, 1, 5, 2, 6, 3, 7)


def scatter_pack(rows):
    blocks = rows.reshape(X_SIZE, 2, -1, rows.shape[-1])
    total = blocks[0].astype(f32)
    for m in range(1, X_SIZE):
        total = total + swap(blocks[m], "fsdp", m).astype(f32)
    return total[0] + swap(total[1].astype(bf16), "fsdp", 4).astype(f32)


def x_groups():
    return [[z * X_SIZE + x for x in range(X_SIZE)] for z in range(2)]


def sum_over_x(rows):
    return lax.psum_scatter(
        rows, "fsdp", scatter_dimension=0, tiled=True, axis_index_groups=x_groups()
    )


def finish_sum(pair):
    mine_first = lax.axis_index("fsdp") < X_SIZE
    own = jnp.where(mine_first, pair[0], pair[1])
    away = jnp.where(mine_first, pair[1], pair[0])
    total = own.astype(f32) + swap(away, "fsdp", 4).astype(f32)
    total = total.astype(bf16)
    total = (total.astype(f32) + swap(total, "rep", 2).astype(f32)).astype(bf16)
    parts = [total] + [swap(total, "rep", 4 * m) for m in range(1, 4)]
    parts = [part.astype(f32) for part in parts]
    return ((parts[0] + parts[1]) + (parts[2] + parts[3])).astype(bf16)


def stacked_heads(array, kv_head):
    first = kv_head * GROUP
    return jnp.concatenate(
        [array[:, (first + g) * HEAD : (first + g + 1) * HEAD] for g in range(GROUP)], axis=0
    )


def attention_forward_kernel(q_ref, kv_ref, key_place_ref, bounds_ref, mixed_ref, log_ref, bias):
    rows = q_ref.shape[0]
    keys = kv_ref.shape[0]
    width = KEY_VALUE_HEADS * HEAD
    place = key_place_ref[...]
    bias[...] = jnp.where(
        (place >= bounds_ref[0:1, :]) & (place <= bounds_ref[1:2, :]), 0.0, masked_score
    )
    for h in range(KEY_VALUE_HEADS):
        queries = stacked_heads(q_ref[...], h)
        keys_h = kv_ref[:, h * HEAD : (h + 1) * HEAD]
        values_h = kv_ref[:, width + h * HEAD : width + (h + 1) * HEAD]
        scores = lax.dot_general(keys_h, queries, NT, preferred_element_type=f32) + bias[...]
        top = jnp.max(scores, axis=0, keepdims=True)
        weights = jnp.exp(scores - top)
        total = jnp.sum(weights, axis=0, keepdims=True)
        mixed = jnp.dot(
            values_h.T, weights.astype(bf16), preferred_element_type=f32
        ) * (1.0 / total)
        mixed = mixed.T.astype(bf16)
        for g in range(GROUP):
            j = h * GROUP + g
            mixed_ref[:, j * HEAD : (j + 1) * HEAD] = mixed[g * rows : (g + 1) * rows]
        log_ref[h : h + 1, :] = top + jnp.log(total)


def attention_backward_kernel(
    q_ref, kv_ref, key_place_ref, bounds_ref, mixed_ref, log_ref, grad_ref, dq_ref, dkv_ref
):
    rows = q_ref.shape[0]
    keys = kv_ref.shape[0]
    width = KEY_VALUE_HEADS * HEAD
    chunk = keys // 4
    for h in range(KEY_VALUE_HEADS):
        queries = stacked_heads(q_ref[...], h)
        grads = stacked_heads(grad_ref[...], h)
        mixed = stacked_heads(mixed_ref[...], h)
        product = (grads.astype(f32) * mixed.astype(f32)).T
        delta = jnp.sum(product, axis=0, keepdims=True)
        logs = log_ref[h : h + 1, :]
        dq = jnp.zeros((HEAD, GROUP * rows), f32)
        for part in range(4):
            span = slice(part * chunk, (part + 1) * chunk)
            place = key_place_ref[span, :]
            allowed = (place >= bounds_ref[0:1, :]) & (place <= bounds_ref[1:2, :])
            keys_h = kv_ref[span, h * HEAD : (h + 1) * HEAD]
            values_h = kv_ref[span, width + h * HEAD : width + (h + 1) * HEAD]
            scores = lax.dot_general(keys_h, queries, NT, preferred_element_type=f32)
            weights = jnp.exp(jnp.where(allowed, scores, masked_score) - logs)
            dweights = lax.dot_general(values_h, grads, NT, preferred_element_type=f32)
            dscores = (weights * (dweights - delta)).astype(bf16)
            dvalues = jnp.dot(weights.astype(bf16), grads, preferred_element_type=f32)
            dkeys = jnp.dot(dscores, queries, preferred_element_type=f32)
            dq = dq + jnp.dot(keys_h.T, dscores, preferred_element_type=f32)
            dkv_ref[span, h * HEAD : (h + 1) * HEAD] = dkeys.astype(bf16)
            dkv_ref[span, width + h * HEAD : width + (h + 1) * HEAD] = dvalues.astype(bf16)
        dq = dq.T * HEAD ** (-0.5)
        for g in range(GROUP):
            j = h * GROUP + g
            dq_ref[:, j * HEAD : (j + 1) * HEAD] = dq[g * rows : (g + 1) * rows]


def kernel_params():
    return pltpu.CompilerParams(vmem_limit_bytes=48 * 1024 * 1024)


def attend(queries, kv, key_place, bounds):
    rows, keys = queries.shape[0], kv.shape[0]
    pairs = QUERY_HEADS * rows * keys
    return pl.pallas_call(
        attention_forward_kernel,
        out_shape=(
            jax.ShapeDtypeStruct(queries.shape, bf16),
            jax.ShapeDtypeStruct((8, GROUP * rows), f32),
        ),
        scratch_shapes=[pltpu.VMEM((keys, GROUP * rows), f32)],
        compiler_params=kernel_params(),
        cost_estimate=pl.CostEstimate(
            flops=4 * pairs * HEAD, bytes_accessed=4 * 1024 * 1024, transcendentals=pairs
        ),
        name="attention_forward",
    )(queries, kv, key_place, bounds)


def attend_back(queries, kv, key_place, bounds, mixed, logs, grads):
    rows, keys = queries.shape[0], kv.shape[0]
    pairs = QUERY_HEADS * rows * keys
    return pl.pallas_call(
        attention_backward_kernel,
        out_shape=(
            jax.ShapeDtypeStruct(queries.shape, f32),
            jax.ShapeDtypeStruct(kv.shape, bf16),
        ),
        compiler_params=kernel_params(),
        cost_estimate=pl.CostEstimate(
            flops=10 * pairs * HEAD, bytes_accessed=6 * 1024 * 1024, transcendentals=pairs
        ),
        name="attention_backward",
    )(queries, kv, key_place, bounds, mixed, logs, grads)


def normalize(stream):
    return stream * lax.rsqrt(jnp.mean(stream * stream, axis=-1, keepdims=True) + epsilon_norm)


def normalize_back(stream, gain, grad):
    inverse = lax.rsqrt(jnp.mean(stream * stream, axis=-1, keepdims=True) + epsilon_norm)
    unit = stream * inverse
    scaled = grad * gain
    gain_grad = jnp.sum(grad * unit, axis=0)
    return inverse * (scaled - unit * jnp.mean(scaled * unit, axis=-1, keepdims=True)), gain_grad


def turn(flat):
    half = HEAD // 2
    ahead = jnp.concatenate([flat[:, half:], flat[:, :half]], axis=1)
    behind = jnp.concatenate([flat[:, -half:], flat[:, :-half]], axis=1)
    lane = lax.broadcasted_iota(jnp.int32, flat.shape, 1) % HEAD
    return jnp.where(lane < half, -ahead, behind)


def rotary(flat, cosine, sine):
    return flat * cosine[:, : flat.shape[1]] + turn(flat) * sine[:, : flat.shape[1]]


def rotary_back(flat, cosine, sine):
    return flat * cosine[:, : flat.shape[1]] - turn(flat * sine[:, : flat.shape[1]])


def matmul(left, right):
    return jnp.dot(left, right, preferred_element_type=f32)


def matmul_nt(left, right):
    return lax.dot_general(left, right, NT, preferred_element_type=f32)


def cross_rows(left, right):
    return lax.dot_general(left, right, (((0,), (0,)), ((), ())), preferred_element_type=f32)


def by_x(columns):
    rows, width = columns.shape
    blocks = columns.reshape(rows, 2, X_SIZE, width // (2 * X_SIZE))
    return blocks.swapaxes(1, 2).reshape(rows, width)


def body(
    tokens,
    seq_lengths,
    attn_gain,
    query_weight,
    key_projection,
    value_projection,
    out_weight,
    mlp_gain,
    gate_weight,
    up_weight,
    down_weight,
    cotangent,
):
    rows, width = tokens.shape
    shard = query_weight.shape[1]
    key_width = key_projection.shape[2]
    att_width = width + key_width
    half_width = width // 2
    me = lax.axis_index("fsdp")
    first_core = lax.axis_index("rep") % 2 == 0

    def pick(a, b):
        return jnp.where(first_core, a, b)

    def gathered(part):
        mine = lax.all_gather(part, "fsdp", axis=0, tiled=True)
        return mine, swap_core(mine)

    layers = []
    for l in range(DECODER_LAYERS):
        gains = jnp.stack([attn_gain[l], mlp_gain[l]])
        gains = jnp.pad(gains, ((0, 6), (0, att_width - shard)))
        own = pick(
            jnp.concatenate([query_weight[l], key_projection[l]], axis=1),
            jnp.concatenate([out_weight[l], value_projection[l]], axis=1),
        )
        mine, other = gathered(jnp.concatenate([own, gains], axis=0))
        blocks = mine.reshape(-1, shard + 8, att_width)
        gain_attn = blocks[:, shard, :shard].reshape(width).astype(f32)
        gain_mlp = blocks[:, shard + 1, :shard].reshape(width).astype(f32)
        mine = blocks[:, :shard].reshape(width, att_width)
        other = other.reshape(-1, shard + 8, att_width)[:, :shard].reshape(width, att_width)
        query_key = pick(mine, other)
        out_value = pick(other, mine)
        gate_up = gathered(pick(gate_weight[l], up_weight[l]))
        down = gathered(pick(down_weight[l][:, :half_width], down_weight[l][:, half_width:]))
        layers.append((gain_attn, gain_mlp, query_key, out_value, gate_up, down))

    lengths = seq_lengths[0]
    ends = jnp.cumsum(lengths)
    starts = ends - lengths
    places = me * rows + jnp.arange(rows, dtype=jnp.int32)
    segment = jnp.sum((places[:, None] >= ends[None, :-1]).astype(jnp.int32), axis=1)
    chosen = segment[:, None] == jnp.arange(lengths.shape[0], dtype=jnp.int32)[None, :]
    start = jnp.sum(chosen.astype(jnp.int32) * starts[None, :], axis=1)
    offsets = (places - start).astype(f32)
    frequency = rope_base ** (-(jnp.arange(HEAD // 2, dtype=f32) * 2.0) / HEAD)
    angles = offsets[:, None] * frequency[None, :]
    cosine = jnp.tile(jnp.cos(angles), (1, 2 * QUERY_HEADS))
    sine = jnp.tile(jnp.sin(angles), (1, 2 * QUERY_HEADS))
    bounds = jnp.stack([jnp.tile(start, GROUP), jnp.tile(places, GROUP)])
    bounds = jnp.pad(bounds, ((0, 6), (0, 0)))
    blocks = jnp.bitwise_xor(me, jnp.array(BLOCK_ORDER, jnp.int32))
    key_place = blocks[:, None] * rows + jnp.arange(rows, dtype=jnp.int32)[None, :]
    key_place = key_place.reshape(-1, 1)

    stream = tokens.astype(f32)
    saved = []
    for l in range(DECODER_LAYERS):
        gain_attn, gain_mlp, query_key, out_value, gate_up, down = layers[l]
        normed = (normalize(stream) * gain_attn).astype(bf16)
        values = matmul(normed, out_value[:, width:]).astype(bf16)
        projected = matmul(normed, query_key)
        keys = rotary(projected[:, width:], cosine, sine).astype(bf16)
        kv = gather_pack(jnp.concatenate([keys, values], axis=1))
        queries = rotary(projected[:, :width], cosine, sine).astype(bf16)
        queries = queries * jnp.asarray(HEAD ** (-0.5), bf16)
        mixed, logs = attend(queries, kv, key_place, bounds)
        middle = stream + matmul(mixed, out_value[:, :width])
        normed_mlp = (normalize(middle) * gain_mlp).astype(bf16)
        mine = matmul(normed_mlp, gate_up[0])
        other = matmul(normed_mlp, gate_up[1])
        gate, up = pick(mine, other), pick(other, mine)
        sigmoid = jax.nn.sigmoid(gate)
        hidden = (gate * sigmoid * up).astype(bf16)
        mine = matmul(hidden, down[0])
        other = matmul(hidden, down[1])
        saved.append((stream, normed, queries, kv, logs, mixed, middle, normed_mlp, gate, up, hidden))
        stream = middle + jnp.concatenate([pick(mine, other), pick(other, mine)], axis=1)
    output = stream.astype(bf16)

    def finish(pair_parts, names):
        widths = [part.shape[-1] for part in pair_parts]
        joined = jnp.concatenate(pair_parts, axis=-1) if len(pair_parts) > 1 else pair_parts[0]
        return finish_sum(joined)

    grad = cotangent.astype(f32)
    results = [None] * DECODER_LAYERS
    for l in reversed(range(DECODER_LAYERS)):
        gain_attn, gain_mlp, query_key, out_value, gate_up, down = layers[l]
        stream, normed, queries, kv, logs, mixed, middle, normed_mlp, gate, up, hidden = saved[l]
        grad_low = grad.astype(bf16)
        grad_a, grad_b = grad_low[:, :half_width], grad_low[:, half_width:]
        grad_mine, grad_other = pick(grad_a, grad_b), pick(grad_b, grad_a)
        hidden_x = by_x(hidden)
        received = swap_core(cross_rows(hidden_x, grad_other).astype(bf16))
        down_sum = (cross_rows(hidden_x, grad_mine) + received.astype(f32)).astype(bf16)
        down_sum = sum_over_x(down_sum)

        dhidden = matmul_nt(grad_mine, down[0]) + matmul_nt(grad_other, down[1])
        sigmoid = jax.nn.sigmoid(gate)
        dgate = (dhidden * up * sigmoid * (1.0 + gate * (1.0 - sigmoid))).astype(bf16)
        dup = (dhidden * gate * sigmoid).astype(bf16)
        dmine, dother = pick(dgate, dup), pick(dup, dgate)
        mlp_x = by_x(normed_mlp)
        received = swap_core(cross_rows(mlp_x, dother).astype(bf16))
        gate_up_sum = (cross_rows(mlp_x, dmine) + received.astype(f32)).astype(bf16)
        gate_up_sum = sum_over_x(gate_up_sum)

        dnormed = matmul_nt(dmine, gate_up[0]) + matmul_nt(dother, gate_up[1])
        dmiddle, mlp_gain_grad = normalize_back(middle, gain_mlp, dnormed)
        dmiddle = dmiddle + grad
        dmiddle_low = dmiddle.astype(bf16)
        dmixed = matmul_nt(dmiddle_low, out_value[:, :width]).astype(bf16)
        dq, dkv = attend_back(queries, kv, key_place, bounds, mixed, logs, dmixed)
        dkv = scatter_pack(dkv)
        dq = rotary_back(dq, cosine, sine).astype(bf16)
        dk = rotary_back(dkv[:, :key_width], cosine, sine).astype(bf16)
        dv = dkv[:, key_width:].astype(bf16)

        dqk = jnp.concatenate([dq, dk], axis=1)
        dnormed = matmul_nt(dqk, query_key) + matmul_nt(dv, out_value[:, width:])
        dstream, attn_gain_grad = normalize_back(stream, gain_attn, dnormed)
        grad = dstream + dmiddle

        normed_x, mixed_x = by_x(normed), by_x(mixed)

        def att_terms(first):
            wide = cross_rows(
                jnp.where(first, normed_x, mixed_x), jnp.where(first, dq, dmiddle_low)
            )
            return jnp.concatenate([wide, cross_rows(normed_x, jnp.where(first, dk, dv))], axis=1)

        received = swap_core(att_terms(jnp.logical_not(first_core)).astype(bf16))
        att_sum = (att_terms(first_core) + received.astype(f32)).astype(bf16)
        gain_grads = jnp.stack([attn_gain_grad, mlp_gain_grad]).astype(bf16)
        received = swap_core(gain_grads)
        gain_grads = by_x((gain_grads.astype(f32) + received.astype(f32)).astype(bf16))
        gain_grads = gain_grads.reshape(2, -1, shard).swapaxes(0, 1)
        gain_grads = jnp.pad(gain_grads, ((0, 0), (0, 6), (0, att_width - shard)))
        att_sum = jnp.concatenate([att_sum.reshape(-1, shard, att_width), gain_grads], axis=1)
        att_sum = sum_over_x(att_sum.reshape(-1, att_width))

        ffn = jnp.concatenate(
            [
                gate_up_sum.reshape(2, shard, -1),
                down_sum.reshape(2, -1, half_width).reshape(2, shard, -1),
            ],
            axis=2,
        )
        ffn = finish_sum(ffn)
        att = finish_sum(att_sum.reshape(2, shard + 8, att_width))
        ffn_other, att_other = swap_core(ffn), swap_core(att)
        ffn_a, ffn_b = pick(ffn, ffn_other), pick(ffn_other, ffn)
        att_a, att_b = pick(att, att_other), pick(att_other, att)
        hidden_width = gate_weight.shape[2]
        down_shape = (down_weight.shape[1], half_width)
        results[l] = (
            att[shard, :shard],
            att_a[:shard, :width],
            att_a[:shard, width:],
            att_b[:shard, width:],
            att_b[:shard, :width],
            att[shard + 1, :shard],
            ffn_a[:, :hidden_width],
            ffn_b[:, :hidden_width],
            jnp.concatenate(
                [
                    ffn_a[:, hidden_width:].reshape(down_shape),
                    ffn_b[:, hidden_width:].reshape(down_shape),
                ],
                axis=1,
            ),
        )
    stacked = [
        jnp.stack([results[l][m].astype(f32) for l in range(DECODER_LAYERS)], axis=0)
        for m in range(9)
    ]
    return (output, grad, *stacked)


def solution(mesh):
    weights = P(None, "fsdp", None)
    gains = P(None, "fsdp")
    packed = P(("rep", "fsdp"), None)
    in_specs = (
        packed,
        P("rep", None),
        gains,
        weights,
        weights,
        weights,
        weights,
        gains,
        weights,
        weights,
        weights,
        packed,
    )
    out_specs = (
        packed,
        packed,
        gains,
        weights,
        weights,
        weights,
        weights,
        gains,
        weights,
        weights,
        weights,
    )
    return jax.shard_map(body, mesh=mesh, in_specs=in_specs, out_specs=out_specs, check_vma=False)
```

```python
import functools

import jax
import jax.numpy as jnp
from jax import lax
from jax.experimental import pallas as pl
from jax.experimental.pallas import tpu as pltpu
from jax.sharding import PartitionSpec as P

QUERY_HEADS = 15
KEY_VALUE_HEADS = 5
GROUP = QUERY_HEADS // KEY_VALUE_HEADS
HEAD = 64
DECODER_LAYERS = 2
X_SIZE = 4

epsilon_norm = 1e-05
rope_base = 100000.0
masked_score = -1e30

f32 = jnp.float32
bf16 = jnp.bfloat16

NT = (((1,), (1,)), ((), ()))


def swap(array, axis, mask):
    count = lax.axis_size(axis)
    return lax.ppermute(array, axis, [(i, i ^ mask) for i in range(count)])


def swap_core(array):
    return swap(array, "rep", 1)


def gather_pack(rows):
    pair = jnp.stack([rows, swap(rows, "fsdp", 4)])
    parts = [pair] + [swap(pair, "fsdp", m) for m in range(1, X_SIZE)]
    return jnp.concatenate(parts, axis=0).reshape(-1, rows.shape[-1])


BLOCK_ORDER = (0, 4, 1, 5, 2, 6, 3, 7)


def scatter_pack(rows):
    blocks = rows.reshape(X_SIZE, 2, -1, rows.shape[-1])
    total = blocks[0].astype(f32)
    for m in range(1, X_SIZE):
        total = total + swap(blocks[m], "fsdp", m).astype(f32)
    return total[0] + swap(total[1].astype(bf16), "fsdp", 4).astype(f32)


def x_groups():
    return [[z * X_SIZE + x for x in range(X_SIZE)] for z in range(2)]


def sum_over_x(rows):
    return lax.psum_scatter(
        rows, "fsdp", scatter_dimension=0, tiled=True, axis_index_groups=x_groups()
    )


def to_owners(pair):
    z_hi = lax.axis_index("fsdp") // X_SIZE
    even = jnp.where(z_hi == 0, pair[0], pair[1])
    odd = jnp.where(z_hi == 0, pair[1], pair[0])
    reps, count = lax.axis_size("rep"), lax.axis_size("fsdp")

    def send(block, flip, z_lo):
        moves = []
        for rep in range(reps):
            for f in range(count):
                owner = 2 * (f % X_SIZE) + ((f // X_SIZE) ^ flip)
                moves.append((rep * count + f, (rep ^ (2 * z_lo)) * count + owner))
        return lax.ppermute(block, ("rep", "fsdp"), moves).astype(f32)

    near = send(even, 0, 0) + send(odd, 1, 0)
    far = send(even, 0, 1) + send(odd, 1, 1)
    return (near + far).astype(bf16)


def finish_sum(pair):
    total = to_owners(pair)
    parts = [total] + [swap(total, "rep", 4 * m) for m in range(1, 4)]
    parts = [part.astype(f32) for part in parts]
    return ((parts[0] + parts[1]) + (parts[2] + parts[3])).astype(bf16)


def assemble_kernel(count, y_parts, *refs):
    parts, out, sems = refs[:count], refs[count], refs[count + 1]
    me = lax.axis_index("fsdp")
    copies = []
    if y_parts:
        y = lax.axis_index("rep") // 4
        columns = parts[0].shape[-1]
        for m in range(count):
            first = pl.multiple_of(jnp.bitwise_xor(y, m) * columns, 128)
            for k, block in enumerate(BLOCK_ORDER):
                place = out.at[jnp.bitwise_xor(me, block), :, pl.ds(first, columns)]
                copies.append((parts[m].at[k], place))
    else:
        for k, block in enumerate(BLOCK_ORDER):
            copies.append((parts[k // 2].at[k % 2], out.at[jnp.bitwise_xor(me, block)]))
    copies = [
        pltpu.make_async_copy(source, place, sems.at[i])
        for i, (source, place) in enumerate(copies)
    ]
    for copy in copies:
        copy.start()
    for copy in copies:
        copy.wait()


def assemble(parts, y_parts):
    rows, columns = parts[0].shape[1:]
    blocks = len(BLOCK_ORDER)
    columns = columns * len(parts) if y_parts else columns
    size = blocks * rows * columns * 4
    return pl.pallas_call(
        functools.partial(assemble_kernel, len(parts), y_parts),
        out_shape=jax.ShapeDtypeStruct((blocks, rows, columns), parts[0].dtype),
        in_specs=[pl.BlockSpec(memory_space=pl.ANY)] * len(parts),
        out_specs=pl.BlockSpec(memory_space=pl.ANY),
        scratch_shapes=[pltpu.SemaphoreType.DMA((blocks * (len(parts) if y_parts else 1),))],
        cost_estimate=pl.CostEstimate(flops=0, bytes_accessed=size, transcendentals=0),
        name="assemble",
    )(*parts)


def gather_blocks(part):
    pair = jnp.stack([part, swap(part, "fsdp", 4)])
    return [pair] + [swap(pair, "fsdp", m) for m in range(1, X_SIZE)]


def gather_by_y(part):
    columns = part.shape[1] // 4
    y = lax.axis_index("rep") // 4
    quarter = lax.dynamic_slice_in_dim(part, y * columns, columns, axis=1)
    blocks = gather_blocks(quarter)
    joined = jnp.concatenate(blocks, axis=0)
    parts = [joined] + [swap(joined, "rep", 4 * m) for m in range(1, 4)]
    return parts, blocks


def stacked_heads(array, kv_head):
    first = kv_head * GROUP
    return jnp.concatenate(
        [array[:, (first + g) * HEAD : (first + g + 1) * HEAD] for g in range(GROUP)], axis=0
    )


def attention_forward_kernel(q_ref, kv_ref, key_place_ref, bounds_ref, mixed_ref, log_ref, bias):
    rows = q_ref.shape[0]
    keys = kv_ref.shape[0]
    width = KEY_VALUE_HEADS * HEAD
    place = key_place_ref[...]
    bias[...] = jnp.where(
        (place >= bounds_ref[0:1, :]) & (place <= bounds_ref[1:2, :]), 0.0, masked_score
    )
    for h in range(KEY_VALUE_HEADS):
        queries = stacked_heads(q_ref[...], h)
        keys_h = kv_ref[:, h * HEAD : (h + 1) * HEAD]
        values_h = kv_ref[:, width + h * HEAD : width + (h + 1) * HEAD]
        scores = lax.dot_general(keys_h, queries, NT, preferred_element_type=f32) + bias[...]
        top = jnp.max(scores, axis=0, keepdims=True)
        weights = jnp.exp(scores - top)
        total = jnp.sum(weights, axis=0, keepdims=True)
        mixed = jnp.dot(
            values_h.T, weights.astype(bf16), preferred_element_type=f32
        ) * (1.0 / total)
        mixed = mixed.T.astype(bf16)
        for g in range(GROUP):
            j = h * GROUP + g
            mixed_ref[:, j * HEAD : (j + 1) * HEAD] = mixed[g * rows : (g + 1) * rows]
        log_ref[h : h + 1, :] = top + jnp.log(total)


def attention_backward_kernel(
    q_ref, kv_ref, key_place_ref, bounds_ref, mixed_ref, log_ref, grad_ref, dq_ref, dkv_ref
):
    rows = q_ref.shape[0]
    keys = kv_ref.shape[0]
    width = KEY_VALUE_HEADS * HEAD
    chunk = keys // 4
    for h in range(KEY_VALUE_HEADS):
        queries = stacked_heads(q_ref[...], h)
        grads = stacked_heads(grad_ref[...], h)
        mixed = stacked_heads(mixed_ref[...], h)
        product = (grads.astype(f32) * mixed.astype(f32)).T
        delta = jnp.sum(product, axis=0, keepdims=True)
        logs = log_ref[h : h + 1, :]
        dq = jnp.zeros((HEAD, GROUP * rows), f32)
        for part in range(4):
            span = slice(part * chunk, (part + 1) * chunk)
            place = key_place_ref[span, :]
            allowed = (place >= bounds_ref[0:1, :]) & (place <= bounds_ref[1:2, :])
            keys_h = kv_ref[span, h * HEAD : (h + 1) * HEAD]
            values_h = kv_ref[span, width + h * HEAD : width + (h + 1) * HEAD]
            scores = lax.dot_general(keys_h, queries, NT, preferred_element_type=f32)
            weights = jnp.exp(jnp.where(allowed, scores, masked_score) - logs)
            dweights = lax.dot_general(values_h, grads, NT, preferred_element_type=f32)
            dscores = (weights * (dweights - delta)).astype(bf16)
            dvalues = jnp.dot(weights.astype(bf16), grads, preferred_element_type=f32)
            dkeys = jnp.dot(dscores, queries, preferred_element_type=f32)
            dq = dq + jnp.dot(keys_h.T, dscores, preferred_element_type=f32)
            dkv_ref[span, h * HEAD : (h + 1) * HEAD] = dkeys.astype(bf16)
            dkv_ref[span, width + h * HEAD : width + (h + 1) * HEAD] = dvalues.astype(bf16)
        dq = dq.T * HEAD ** (-0.5)
        for g in range(GROUP):
            j = h * GROUP + g
            dq_ref[:, j * HEAD : (j + 1) * HEAD] = dq[g * rows : (g + 1) * rows]


def kernel_params():
    return pltpu.CompilerParams(vmem_limit_bytes=48 * 1024 * 1024)


def attend(queries, kv, key_place, bounds):
    rows, keys = queries.shape[0], kv.shape[0]
    pairs = QUERY_HEADS * rows * keys
    return pl.pallas_call(
        attention_forward_kernel,
        out_shape=(
            jax.ShapeDtypeStruct(queries.shape, bf16),
            jax.ShapeDtypeStruct((8, GROUP * rows), f32),
        ),
        scratch_shapes=[pltpu.VMEM((keys, GROUP * rows), f32)],
        compiler_params=kernel_params(),
        cost_estimate=pl.CostEstimate(
            flops=4 * pairs * HEAD, bytes_accessed=4 * 1024 * 1024, transcendentals=pairs
        ),
        name="attention_forward",
    )(queries, kv, key_place, bounds)


def attend_back(queries, kv, key_place, bounds, mixed, logs, grads):
    rows, keys = queries.shape[0], kv.shape[0]
    pairs = QUERY_HEADS * rows * keys
    return pl.pallas_call(
        attention_backward_kernel,
        out_shape=(
            jax.ShapeDtypeStruct(queries.shape, f32),
            jax.ShapeDtypeStruct(kv.shape, bf16),
        ),
        compiler_params=kernel_params(),
        cost_estimate=pl.CostEstimate(
            flops=10 * pairs * HEAD, bytes_accessed=6 * 1024 * 1024, transcendentals=pairs
        ),
        name="attention_backward",
    )(queries, kv, key_place, bounds, mixed, logs, grads)


def normalize(stream):
    return stream * lax.rsqrt(jnp.mean(stream * stream, axis=-1, keepdims=True) + epsilon_norm)


def normalize_back(stream, gain, grad):
    inverse = lax.rsqrt(jnp.mean(stream * stream, axis=-1, keepdims=True) + epsilon_norm)
    unit = stream * inverse
    scaled = grad * gain
    gain_grad = jnp.sum(grad * unit, axis=0)
    return inverse * (scaled - unit * jnp.mean(scaled * unit, axis=-1, keepdims=True)), gain_grad


def turn(flat):
    half = HEAD // 2
    ahead = jnp.concatenate([flat[:, half:], flat[:, :half]], axis=1)
    behind = jnp.concatenate([flat[:, -half:], flat[:, :-half]], axis=1)
    lane = lax.broadcasted_iota(jnp.int32, flat.shape, 1) % HEAD
    return jnp.where(lane < half, -ahead, behind)


def rotary(flat, cosine, sine):
    return flat * cosine[:, : flat.shape[1]] + turn(flat) * sine[:, : flat.shape[1]]


def rotary_back(flat, cosine, sine):
    return flat * cosine[:, : flat.shape[1]] - turn(flat * sine[:, : flat.shape[1]])


def matmul(left, right):
    return jnp.dot(left, right, preferred_element_type=f32)


def matmul_nt(left, right):
    return lax.dot_general(left, right, NT, preferred_element_type=f32)


def cross_rows(left, right):
    return lax.dot_general(left, right, (((0,), (0,)), ((), ())), preferred_element_type=f32)


def body(
    tokens,
    seq_lengths,
    attn_gain,
    query_weight,
    key_projection,
    value_projection,
    out_weight,
    mlp_gain,
    gate_weight,
    up_weight,
    down_weight,
    cotangent,
):
    rows, width = tokens.shape
    shard = query_weight.shape[1]
    key_width = key_projection.shape[2]
    att_width = width + key_width
    half_width = width // 2
    me = lax.axis_index("fsdp")
    first_core = lax.axis_index("rep") % 2 == 0

    def pick(a, b):
        return jnp.where(first_core, a, b)

    def after(part, earlier):
        return lax.optimization_barrier((part, earlier))[0]

    layers = []
    last = None
    for l in range(DECODER_LAYERS):
        gains = jnp.stack([attn_gain[l], mlp_gain[l]])
        gains = jnp.pad(gains, ((0, 6), (0, att_width - shard)))
        att = pick(
            jnp.concatenate([query_weight[l], key_projection[l]], axis=1),
            jnp.concatenate([out_weight[l], value_projection[l]], axis=1),
        )
        att = jnp.concatenate([att, gains], axis=0)
        gate_up = pick(gate_weight[l], up_weight[l])
        down = pick(down_weight[l][:, :half_width], down_weight[l][:, half_width:])

        if last is not None:
            gate_up = after(gate_up, last[-1])
        by_y, last = gather_by_y(gate_up)
        att_parts = gather_blocks(after(att, last[-1]))
        down_parts = gather_blocks(after(down, att_parts[-1]))
        last = down_parts

        mine = assemble(att_parts, False)
        other = swap_core(mine)
        gain_attn = mine[:, shard, :shard].reshape(width).astype(f32)
        gain_mlp = mine[:, shard + 1, :shard].reshape(width).astype(f32)
        mine = mine[:, :shard].reshape(width, att_width)
        other = other[:, :shard].reshape(width, att_width)
        query_key = pick(mine, other)
        out_value = pick(other, mine)
        mine = assemble(by_y, True).reshape(width, -1)
        gate_up = (mine, swap_core(mine))
        mine = assemble(down_parts, False).reshape(-1, half_width)
        down = (mine, swap_core(mine))
        layers.append((gain_attn, gain_mlp, query_key, out_value, gate_up, down))

    lengths = seq_lengths[0]
    ends = jnp.cumsum(lengths)
    starts = ends - lengths
    places = me * rows + jnp.arange(rows, dtype=jnp.int32)
    segment = jnp.sum((places[:, None] >= ends[None, :-1]).astype(jnp.int32), axis=1)
    chosen = segment[:, None] == jnp.arange(lengths.shape[0], dtype=jnp.int32)[None, :]
    start = jnp.sum(chosen.astype(jnp.int32) * starts[None, :], axis=1)
    offsets = (places - start).astype(f32)
    frequency = rope_base ** (-(jnp.arange(HEAD // 2, dtype=f32) * 2.0) / HEAD)
    angles = offsets[:, None] * frequency[None, :]
    cosine = jnp.tile(jnp.cos(angles), (1, 2 * QUERY_HEADS))
    sine = jnp.tile(jnp.sin(angles), (1, 2 * QUERY_HEADS))
    bounds = jnp.stack([jnp.tile(start, GROUP), jnp.tile(places, GROUP)])
    bounds = jnp.pad(bounds, ((0, 6), (0, 0)))
    blocks = jnp.bitwise_xor(me, jnp.array(BLOCK_ORDER, jnp.int32))
    key_place = blocks[:, None] * rows + jnp.arange(rows, dtype=jnp.int32)[None, :]
    key_place = key_place.reshape(-1, 1)

    stream = tokens.astype(f32)
    saved = []
    for l in range(DECODER_LAYERS):
        gain_attn, gain_mlp, query_key, out_value, gate_up, down = layers[l]
        normed = (normalize(stream) * gain_attn).astype(bf16)
        values = matmul(normed, out_value[:, width:]).astype(bf16)
        projected = matmul(normed, query_key)
        keys = rotary(projected[:, width:], cosine, sine).astype(bf16)
        kv = gather_pack(jnp.concatenate([keys, values], axis=1))
        queries = rotary(projected[:, :width], cosine, sine).astype(bf16)
        queries = queries * jnp.asarray(HEAD ** (-0.5), bf16)
        mixed, logs = attend(queries, kv, key_place, bounds)
        middle = stream + matmul(mixed, out_value[:, :width])
        normed_mlp = (normalize(middle) * gain_mlp).astype(bf16)
        mine = matmul(normed_mlp, gate_up[0])
        other = matmul(normed_mlp, gate_up[1])
        gate, up = pick(mine, other), pick(other, mine)
        sigmoid = jax.nn.sigmoid(gate)
        hidden = (gate * sigmoid * up).astype(bf16)
        mine = matmul(hidden, down[0])
        other = matmul(hidden, down[1])
        saved.append((stream, normed, queries, kv, logs, mixed, middle, normed_mlp, gate, up, hidden))
        stream = middle + jnp.concatenate([pick(mine, other), pick(other, mine)], axis=1)
    output = stream.astype(bf16)

    grad = cotangent.astype(f32)
    results = [None] * DECODER_LAYERS
    for l in reversed(range(DECODER_LAYERS)):
        gain_attn, gain_mlp, query_key, out_value, gate_up, down = layers[l]
        stream, normed, queries, kv, logs, mixed, middle, normed_mlp, gate, up, hidden = saved[l]
        grad_low = grad.astype(bf16)
        grad_a, grad_b = grad_low[:, :half_width], grad_low[:, half_width:]
        grad_mine, grad_other = pick(grad_a, grad_b), pick(grad_b, grad_a)
        received = swap_core(cross_rows(hidden, grad_other).astype(bf16))
        down_sum = (cross_rows(hidden, grad_mine) + received.astype(f32)).astype(bf16)
        down_sum = sum_over_x(down_sum)

        dhidden = matmul_nt(grad_mine, down[0]) + matmul_nt(grad_other, down[1])
        sigmoid = jax.nn.sigmoid(gate)
        dgate = (dhidden * up * sigmoid * (1.0 + gate * (1.0 - sigmoid))).astype(bf16)
        dup = (dhidden * gate * sigmoid).astype(bf16)
        dmine, dother = pick(dgate, dup), pick(dup, dgate)
        received = swap_core(cross_rows(normed_mlp, dother).astype(bf16))
        gate_up_sum = (cross_rows(normed_mlp, dmine) + received.astype(f32)).astype(bf16)
        gate_up_sum = sum_over_x(gate_up_sum)

        dnormed = matmul_nt(dmine, gate_up[0]) + matmul_nt(dother, gate_up[1])
        dmiddle, mlp_gain_grad = normalize_back(middle, gain_mlp, dnormed)
        dmiddle = dmiddle + grad
        dmiddle_low = dmiddle.astype(bf16)
        dmixed = matmul_nt(dmiddle_low, out_value[:, :width]).astype(bf16)
        dq, dkv = attend_back(queries, kv, key_place, bounds, mixed, logs, dmixed)
        dkv = scatter_pack(dkv)
        dq = rotary_back(dq, cosine, sine).astype(bf16)
        dk = rotary_back(dkv[:, :key_width], cosine, sine).astype(bf16)
        dv = dkv[:, key_width:].astype(bf16)

        dqk = jnp.concatenate([dq, dk], axis=1)
        dnormed = matmul_nt(dqk, query_key) + matmul_nt(dv, out_value[:, width:])
        dstream, attn_gain_grad = normalize_back(stream, gain_attn, dnormed)
        grad = dstream + dmiddle

        def att_terms(first):
            wide = cross_rows(
                jnp.where(first, normed, mixed), jnp.where(first, dq, dmiddle_low)
            )
            return jnp.concatenate([wide, cross_rows(normed, jnp.where(first, dk, dv))], axis=1)

        received = swap_core(att_terms(jnp.logical_not(first_core)).astype(bf16))
        att_sum = (att_terms(first_core) + received.astype(f32)).astype(bf16)
        gain_grads = jnp.stack([attn_gain_grad, mlp_gain_grad]).astype(bf16)
        received = swap_core(gain_grads)
        gain_grads = (gain_grads.astype(f32) + received.astype(f32)).astype(bf16)
        gain_grads = gain_grads.reshape(2, -1, shard).swapaxes(0, 1)
        gain_grads = jnp.pad(gain_grads, ((0, 0), (0, 6), (0, att_width - shard)))
        att_sum = jnp.concatenate([att_sum.reshape(-1, shard, att_width), gain_grads], axis=1)
        att_sum = sum_over_x(att_sum.reshape(-1, att_width))

        def whole(pair):
            own = finish_sum(pair)
            return own, swap_core(own)

        gate_up_own, gate_up_other = whole(gate_up_sum.reshape(2, shard, -1))
        down_own, down_other = whole(down_sum.reshape(2, -1, half_width))
        att_own, att_other = whole(att_sum.reshape(2, shard + 8, att_width))
        att_a, att_b = pick(att_own, att_other), pick(att_other, att_own)
        results[l] = (
            att_own[shard, :shard],
            att_a[:shard, :width],
            att_a[:shard, width:],
            att_b[:shard, width:],
            att_b[:shard, :width],
            att_own[shard + 1, :shard],
            pick(gate_up_own, gate_up_other),
            pick(gate_up_other, gate_up_own),
            jnp.concatenate([pick(down_own, down_other), pick(down_other, down_own)], axis=1),
        )
    stacked = [
        jnp.stack([results[l][m].astype(f32) for l in range(DECODER_LAYERS)], axis=0)
        for m in range(9)
    ]
    return (output, grad, *stacked)


def solution(mesh):
    weights = P(None, "fsdp", None)
    gains = P(None, "fsdp")
    packed = P(("rep", "fsdp"), None)
    in_specs = (
        packed,
        P("rep", None),
        gains,
        weights,
        weights,
        weights,
        weights,
        gains,
        weights,
        weights,
        weights,
        packed,
    )
    out_specs = (
        packed,
        packed,
        gains,
        weights,
        weights,
        weights,
        weights,
        gains,
        weights,
        weights,
        weights,
    )
    return jax.shard_map(body, mesh=mesh, in_specs=in_specs, out_specs=out_specs, check_vma=False)
```

```python
import functools

import jax
import jax.numpy as jnp
from jax import lax
from jax.experimental import pallas as pl
from jax.experimental.pallas import tpu as pltpu
from jax.sharding import PartitionSpec as P

QUERY_HEADS = 15
KEY_VALUE_HEADS = 5
GROUP = QUERY_HEADS // KEY_VALUE_HEADS
HEAD = 64
DECODER_LAYERS = 2
X_SIZE = 4

epsilon_norm = 1e-05
rope_base = 100000.0
masked_score = -1e30

f32 = jnp.float32
bf16 = jnp.bfloat16

NT = (((1,), (1,)), ((), ()))


def swap(array, axis, mask):
    count = lax.axis_size(axis)
    return lax.ppermute(array, axis, [(i, i ^ mask) for i in range(count)])


def swap_core(array):
    return swap(array, "rep", 1)


def gather_pack(rows):
    pair = jnp.stack([rows, swap(rows, "fsdp", 4)])
    parts = [pair] + [swap(pair, "fsdp", m) for m in range(1, X_SIZE)]
    return jnp.concatenate(parts, axis=0).reshape(-1, rows.shape[-1])


BLOCK_ORDER = (0, 4, 1, 5, 2, 6, 3, 7)


def scatter_pack(rows):
    blocks = rows.reshape(X_SIZE, 2, -1, rows.shape[-1])
    total = blocks[0].astype(f32)
    for m in range(1, X_SIZE):
        total = total + swap(blocks[m], "fsdp", m).astype(f32)
    return total[0] + swap(total[1].astype(bf16), "fsdp", 4).astype(f32)


def x_groups():
    return [[z * X_SIZE + x for x in range(X_SIZE)] for z in range(2)]


def sum_over_x(rows):
    return lax.psum_scatter(
        rows, "fsdp", scatter_dimension=0, tiled=True, axis_index_groups=x_groups()
    )


def to_owners(pair):
    z_hi = lax.axis_index("fsdp") // X_SIZE
    even = jnp.where(z_hi == 0, pair[0], pair[1])
    odd = jnp.where(z_hi == 0, pair[1], pair[0])
    reps, count = lax.axis_size("rep"), lax.axis_size("fsdp")

    def send(block, flip, z_lo):
        moves = []
        for rep in range(reps):
            for f in range(count):
                owner = 2 * (f % X_SIZE) + ((f // X_SIZE) ^ flip)
                moves.append((rep * count + f, (rep ^ (2 * z_lo)) * count + owner))
        return lax.ppermute(block, ("rep", "fsdp"), moves).astype(f32)

    near = send(even, 0, 0) + send(odd, 1, 0)
    far = send(even, 0, 1) + send(odd, 1, 1)
    return (near + far).astype(bf16)


def finish_sum(pair):
    total = to_owners(pair)
    parts = [total] + [swap(total, "rep", 4 * m) for m in range(1, 4)]
    parts = [part.astype(f32) for part in parts]
    return ((parts[0] + parts[1]) + (parts[2] + parts[3])).astype(bf16)


def kernel_params():
    return pltpu.CompilerParams(vmem_limit_bytes=48 * 1024 * 1024)


def assemble_kernel(count, y_parts, *refs):
    parts, out, sems = refs[:count], refs[count], refs[count + 1]
    me = lax.axis_index("fsdp")
    copies = []
    if y_parts:
        y = lax.axis_index("rep") // 4
        columns = parts[0].shape[-1]
        for m in range(count):
            first = pl.multiple_of(jnp.bitwise_xor(y, m) * columns, 128)
            for k, block in enumerate(BLOCK_ORDER):
                place = out.at[jnp.bitwise_xor(me, block), :, pl.ds(first, columns)]
                copies.append((parts[m].at[k], place))
    else:
        for k, block in enumerate(BLOCK_ORDER):
            copies.append((parts[k // 2].at[k % 2], out.at[jnp.bitwise_xor(me, block)]))
    copies = [
        pltpu.make_async_copy(source, place, sems.at[i])
        for i, (source, place) in enumerate(copies)
    ]
    for copy in copies:
        copy.start()
    for copy in copies:
        copy.wait()


def assemble(parts, y_parts):
    rows, columns = parts[0].shape[1:]
    blocks = len(BLOCK_ORDER)
    columns = columns * len(parts) if y_parts else columns
    size = blocks * rows * columns * 4
    return pl.pallas_call(
        functools.partial(assemble_kernel, len(parts), y_parts),
        out_shape=jax.ShapeDtypeStruct((blocks, rows, columns), parts[0].dtype),
        in_specs=[pl.BlockSpec(memory_space=pl.ANY)] * len(parts),
        out_specs=pl.BlockSpec(memory_space=pltpu.VMEM),
        compiler_params=kernel_params(),
        scratch_shapes=[pltpu.SemaphoreType.DMA((blocks * (len(parts) if y_parts else 1),))],
        cost_estimate=pl.CostEstimate(flops=0, bytes_accessed=size, transcendentals=0),
        name="assemble",
    )(*parts)


def after(array, earlier):
    return lax.optimization_barrier((array, earlier))[0]


def gather_blocks(part, earlier):
    pair = jnp.stack([part, swap(part, "fsdp", 4)])
    pair = pair if earlier is None else after(pair, earlier)
    return [pair] + [swap(pair, "fsdp", m) for m in range(1, X_SIZE)]


def gather_by_y(part, earlier):
    columns = part.shape[1] // 4
    y = lax.axis_index("rep") // 4
    quarter = lax.dynamic_slice_in_dim(part, y * columns, columns, axis=1)
    blocks = gather_blocks(quarter, earlier)
    joined = jnp.concatenate(blocks, axis=0)
    parts = [joined] + [swap(joined, "rep", 4 * m) for m in range(1, 4)]
    return parts, blocks


def stacked_heads(array, kv_head):
    first = kv_head * GROUP
    return jnp.concatenate(
        [array[:, (first + g) * HEAD : (first + g + 1) * HEAD] for g in range(GROUP)], axis=0
    )


def attention_forward_kernel(q_ref, kv_ref, key_place_ref, bounds_ref, mixed_ref, log_ref, bias):
    rows = q_ref.shape[0]
    keys = kv_ref.shape[0]
    width = KEY_VALUE_HEADS * HEAD
    place = key_place_ref[...]
    bias[...] = jnp.where(
        (place >= bounds_ref[0:1, :]) & (place <= bounds_ref[1:2, :]), 0.0, masked_score
    )
    for h in range(KEY_VALUE_HEADS):
        queries = stacked_heads(q_ref[...], h)
        keys_h = kv_ref[:, h * HEAD : (h + 1) * HEAD]
        values_h = kv_ref[:, width + h * HEAD : width + (h + 1) * HEAD]
        scores = lax.dot_general(keys_h, queries, NT, preferred_element_type=f32) + bias[...]
        top = jnp.max(scores, axis=0, keepdims=True)
        weights = jnp.exp(scores - top)
        total = jnp.sum(weights, axis=0, keepdims=True)
        mixed = jnp.dot(
            values_h.T, weights.astype(bf16), preferred_element_type=f32
        ) * (1.0 / total)
        mixed = mixed.T.astype(bf16)
        for g in range(GROUP):
            j = h * GROUP + g
            mixed_ref[:, j * HEAD : (j + 1) * HEAD] = mixed[g * rows : (g + 1) * rows]
        log_ref[h : h + 1, :] = top + jnp.log(total)


def attention_backward_kernel(
    q_ref, kv_ref, key_place_ref, bounds_ref, mixed_ref, log_ref, grad_ref, dq_ref, dkv_ref
):
    rows = q_ref.shape[0]
    keys = kv_ref.shape[0]
    width = KEY_VALUE_HEADS * HEAD
    chunk = keys // 4
    for h in range(KEY_VALUE_HEADS):
        queries = stacked_heads(q_ref[...], h)
        grads = stacked_heads(grad_ref[...], h)
        mixed = stacked_heads(mixed_ref[...], h)
        product = (grads.astype(f32) * mixed.astype(f32)).T
        delta = jnp.sum(product, axis=0, keepdims=True)
        logs = log_ref[h : h + 1, :]
        dq = jnp.zeros((HEAD, GROUP * rows), f32)
        for part in range(4):
            span = slice(part * chunk, (part + 1) * chunk)
            place = key_place_ref[span, :]
            allowed = (place >= bounds_ref[0:1, :]) & (place <= bounds_ref[1:2, :])
            keys_h = kv_ref[span, h * HEAD : (h + 1) * HEAD]
            values_h = kv_ref[span, width + h * HEAD : width + (h + 1) * HEAD]
            scores = lax.dot_general(keys_h, queries, NT, preferred_element_type=f32)
            weights = jnp.exp(jnp.where(allowed, scores, masked_score) - logs)
            dweights = lax.dot_general(values_h, grads, NT, preferred_element_type=f32)
            dscores = (weights * (dweights - delta)).astype(bf16)
            dvalues = jnp.dot(weights.astype(bf16), grads, preferred_element_type=f32)
            dkeys = jnp.dot(dscores, queries, preferred_element_type=f32)
            dq = dq + jnp.dot(keys_h.T, dscores, preferred_element_type=f32)
            dkv_ref[span, h * HEAD : (h + 1) * HEAD] = dkeys.astype(bf16)
            dkv_ref[span, width + h * HEAD : width + (h + 1) * HEAD] = dvalues.astype(bf16)
        dq = dq.T * HEAD ** (-0.5)
        for g in range(GROUP):
            j = h * GROUP + g
            dq_ref[:, j * HEAD : (j + 1) * HEAD] = dq[g * rows : (g + 1) * rows]


def attend(queries, kv, key_place, bounds):
    rows, keys = queries.shape[0], kv.shape[0]
    pairs = QUERY_HEADS * rows * keys
    return pl.pallas_call(
        attention_forward_kernel,
        out_shape=(
            jax.ShapeDtypeStruct(queries.shape, bf16),
            jax.ShapeDtypeStruct((8, GROUP * rows), f32),
        ),
        scratch_shapes=[pltpu.VMEM((keys, GROUP * rows), f32)],
        compiler_params=kernel_params(),
        cost_estimate=pl.CostEstimate(
            flops=4 * pairs * HEAD, bytes_accessed=4 * 1024 * 1024, transcendentals=pairs
        ),
        name="attention_forward",
    )(queries, kv, key_place, bounds)


def attend_back(queries, kv, key_place, bounds, mixed, logs, grads):
    rows, keys = queries.shape[0], kv.shape[0]
    pairs = QUERY_HEADS * rows * keys
    return pl.pallas_call(
        attention_backward_kernel,
        out_shape=(
            jax.ShapeDtypeStruct(queries.shape, f32),
            jax.ShapeDtypeStruct(kv.shape, bf16),
        ),
        compiler_params=kernel_params(),
        cost_estimate=pl.CostEstimate(
            flops=10 * pairs * HEAD, bytes_accessed=6 * 1024 * 1024, transcendentals=pairs
        ),
        name="attention_backward",
    )(queries, kv, key_place, bounds, mixed, logs, grads)


def normalize(stream):
    return stream * lax.rsqrt(jnp.mean(stream * stream, axis=-1, keepdims=True) + epsilon_norm)


def normalize_back(stream, gain, grad):
    inverse = lax.rsqrt(jnp.mean(stream * stream, axis=-1, keepdims=True) + epsilon_norm)
    unit = stream * inverse
    scaled = grad * gain
    gain_grad = jnp.sum(grad * unit, axis=0)
    return inverse * (scaled - unit * jnp.mean(scaled * unit, axis=-1, keepdims=True)), gain_grad


def turn(flat):
    half = HEAD // 2
    ahead = jnp.concatenate([flat[:, half:], flat[:, :half]], axis=1)
    behind = jnp.concatenate([flat[:, -half:], flat[:, :-half]], axis=1)
    lane = lax.broadcasted_iota(jnp.int32, flat.shape, 1) % HEAD
    return jnp.where(lane < half, -ahead, behind)


def rotary(flat, cosine, sine):
    return flat * cosine[:, : flat.shape[1]] + turn(flat) * sine[:, : flat.shape[1]]


def rotary_back(flat, cosine, sine):
    return flat * cosine[:, : flat.shape[1]] - turn(flat * sine[:, : flat.shape[1]])


def matmul(left, right):
    return jnp.dot(left, right, preferred_element_type=f32)


def matmul_nt(left, right):
    return lax.dot_general(left, right, NT, preferred_element_type=f32)


def cross_rows(left, right):
    return lax.dot_general(left, right, (((0,), (0,)), ((), ())), preferred_element_type=f32)


def body(
    tokens,
    seq_lengths,
    attn_gain,
    query_weight,
    key_projection,
    value_projection,
    out_weight,
    mlp_gain,
    gate_weight,
    up_weight,
    down_weight,
    cotangent,
):
    rows, width = tokens.shape
    shard = query_weight.shape[1]
    key_width = key_projection.shape[2]
    att_width = width + key_width
    half_width = width // 2
    me = lax.axis_index("fsdp")
    first_core = lax.axis_index("rep") % 2 == 0

    def pick(a, b):
        return jnp.where(first_core, a, b)

    lengths = seq_lengths[0]
    ends = jnp.cumsum(lengths)
    starts = ends - lengths
    places = me * rows + jnp.arange(rows, dtype=jnp.int32)
    segment = jnp.sum((places[:, None] >= ends[None, :-1]).astype(jnp.int32), axis=1)
    chosen = segment[:, None] == jnp.arange(lengths.shape[0], dtype=jnp.int32)[None, :]
    start = jnp.sum(chosen.astype(jnp.int32) * starts[None, :], axis=1)
    offsets = (places - start).astype(f32)
    frequency = rope_base ** (-(jnp.arange(HEAD // 2, dtype=f32) * 2.0) / HEAD)
    angles = offsets[:, None] * frequency[None, :]
    cosine = jnp.tile(jnp.cos(angles), (1, 2 * QUERY_HEADS))
    sine = jnp.tile(jnp.sin(angles), (1, 2 * QUERY_HEADS))
    bounds = jnp.stack([jnp.tile(start, GROUP), jnp.tile(places, GROUP)])
    bounds = jnp.pad(bounds, ((0, 6), (0, 0)))
    blocks = jnp.bitwise_xor(me, jnp.array(BLOCK_ORDER, jnp.int32))
    key_place = blocks[:, None] * rows + jnp.arange(rows, dtype=jnp.int32)[None, :]
    key_place = key_place.reshape(-1, 1)

    def own_weights(l):
        gains = jnp.stack([attn_gain[l], mlp_gain[l]])
        gains = jnp.pad(gains, ((0, 6), (0, att_width - shard)))
        att = pick(
            jnp.concatenate([query_weight[l], key_projection[l]], axis=1),
            jnp.concatenate([out_weight[l], value_projection[l]], axis=1),
        )
        att = jnp.concatenate([att, gains], axis=0)
        gate_up = pick(gate_weight[l], up_weight[l])
        down = pick(down_weight[l][:, :half_width], down_weight[l][:, half_width:])
        return att, gate_up, down

    def gather_parts(own, earlier):
        att, gate_up, down = own
        by_y, blocks = gather_by_y(gate_up, earlier)
        att_parts = gather_blocks(att, blocks)
        down_parts = gather_blocks(down, att_parts)
        return att_parts, by_y, down_parts

    def whole_weights(parts, earlier):
        att_parts, by_y, down_parts = parts if earlier is None else after(parts, earlier)
        mine = assemble(att_parts, False)
        other = swap_core(mine)
        gain_attn = mine[:, shard, :shard].reshape(width).astype(f32)
        gain_mlp = mine[:, shard + 1, :shard].reshape(width).astype(f32)
        mine = mine[:, :shard].reshape(width, att_width)
        other = other[:, :shard].reshape(width, att_width)
        query_key = pick(mine, other)
        out_value = pick(other, mine)
        mine = assemble(by_y, True).reshape(width, -1)
        gate_up = (mine, swap_core(mine))
        mine = assemble(down_parts, False).reshape(-1, half_width)
        down = (mine, swap_core(mine))
        return gain_attn, gain_mlp, query_key, out_value, gate_up, down

    stream = tokens.astype(f32)
    saved = []
    parts = gather_parts(own_weights(0), None)
    layers = [whole_weights(parts, None)]
    for l in range(DECODER_LAYERS):
        gain_attn, gain_mlp, query_key, out_value, gate_up, down = layers[l]
        normed = (normalize(stream) * gain_attn).astype(bf16)
        values = matmul(normed, out_value[:, width:]).astype(bf16)
        projected = matmul(normed, query_key)
        if l + 1 < DECODER_LAYERS:
            parts = gather_parts(own_weights(l + 1), (parts, projected))
        keys = rotary(projected[:, width:], cosine, sine).astype(bf16)
        kv = gather_pack(jnp.concatenate([keys, values], axis=1))
        queries = rotary(projected[:, :width], cosine, sine).astype(bf16)
        queries = queries * jnp.asarray(HEAD ** (-0.5), bf16)
        mixed, logs = attend(queries, kv, key_place, bounds)
        if l + 1 < DECODER_LAYERS:
            layers.append(whole_weights(parts, mixed))
        middle = stream + matmul(mixed, out_value[:, :width])
        normed_mlp = (normalize(middle) * gain_mlp).astype(bf16)
        mine = matmul(normed_mlp, gate_up[0])
        other = matmul(normed_mlp, gate_up[1])
        gate, up = pick(mine, other), pick(other, mine)
        sigmoid = jax.nn.sigmoid(gate)
        hidden = (gate * sigmoid * up).astype(bf16)
        mine = matmul(hidden, down[0])
        other = matmul(hidden, down[1])
        saved.append((stream, normed, queries, kv, logs, mixed, middle, normed_mlp, gate, up, hidden))
        stream = middle + jnp.concatenate([pick(mine, other), pick(other, mine)], axis=1)
    output = stream.astype(bf16)

    earlier = output

    def next_sum(rows):
        nonlocal earlier
        earlier = sum_over_x(after(rows, earlier))
        return earlier

    grad = cotangent.astype(f32)
    results = [None] * DECODER_LAYERS
    for l in reversed(range(DECODER_LAYERS)):
        gain_attn, gain_mlp, query_key, out_value, gate_up, down = layers[l]
        stream, normed, queries, kv, logs, mixed, middle, normed_mlp, gate, up, hidden = saved[l]
        grad_low = grad.astype(bf16)
        grad_a, grad_b = grad_low[:, :half_width], grad_low[:, half_width:]
        grad_mine, grad_other = pick(grad_a, grad_b), pick(grad_b, grad_a)
        received = swap_core(cross_rows(hidden, grad_other).astype(bf16))
        down_sum = (cross_rows(hidden, grad_mine) + received.astype(f32)).astype(bf16)
        down_sum = next_sum(down_sum)

        dhidden = matmul_nt(grad_mine, down[0]) + matmul_nt(grad_other, down[1])
        sigmoid = jax.nn.sigmoid(gate)
        dgate = (dhidden * up * sigmoid * (1.0 + gate * (1.0 - sigmoid))).astype(bf16)
        dup = (dhidden * gate * sigmoid).astype(bf16)
        dmine, dother = pick(dgate, dup), pick(dup, dgate)
        received = swap_core(cross_rows(normed_mlp, dother).astype(bf16))
        gate_up_sum = (cross_rows(normed_mlp, dmine) + received.astype(f32)).astype(bf16)
        gate_up_sum = next_sum(gate_up_sum)

        dnormed = matmul_nt(dmine, gate_up[0]) + matmul_nt(dother, gate_up[1])
        dmiddle, mlp_gain_grad = normalize_back(middle, gain_mlp, dnormed)
        dmiddle = dmiddle + grad
        dmiddle_low = dmiddle.astype(bf16)
        dmixed = matmul_nt(dmiddle_low, out_value[:, :width]).astype(bf16)
        dq, dkv = attend_back(queries, kv, key_place, bounds, mixed, logs, dmixed)
        dkv = scatter_pack(dkv)
        dq = rotary_back(dq, cosine, sine).astype(bf16)
        dk = rotary_back(dkv[:, :key_width], cosine, sine).astype(bf16)
        dv = dkv[:, key_width:].astype(bf16)

        dqk = jnp.concatenate([dq, dk], axis=1)
        dnormed = matmul_nt(dqk, query_key) + matmul_nt(dv, out_value[:, width:])
        dstream, attn_gain_grad = normalize_back(stream, gain_attn, dnormed)
        grad = dstream + dmiddle

        def att_terms(first):
            wide = cross_rows(
                jnp.where(first, normed, mixed), jnp.where(first, dq, dmiddle_low)
            )
            return jnp.concatenate([wide, cross_rows(normed, jnp.where(first, dk, dv))], axis=1)

        received = swap_core(att_terms(jnp.logical_not(first_core)).astype(bf16))
        att_sum = (att_terms(first_core) + received.astype(f32)).astype(bf16)
        gain_grads = jnp.stack([attn_gain_grad, mlp_gain_grad]).astype(bf16)
        received = swap_core(gain_grads)
        gain_grads = (gain_grads.astype(f32) + received.astype(f32)).astype(bf16)
        gain_grads = gain_grads.reshape(2, -1, shard).swapaxes(0, 1)
        gain_grads = jnp.pad(gain_grads, ((0, 0), (0, 6), (0, att_width - shard)))
        att_sum = jnp.concatenate([att_sum.reshape(-1, shard, att_width), gain_grads], axis=1)
        att_sum = next_sum(att_sum.reshape(-1, att_width))

        def whole(pair):
            own = finish_sum(pair)
            return own, swap_core(own)

        gate_up_own, gate_up_other = whole(gate_up_sum.reshape(2, shard, -1))
        down_own, down_other = whole(down_sum.reshape(2, -1, half_width))
        att_own, att_other = whole(att_sum.reshape(2, shard + 8, att_width))
        att_a, att_b = pick(att_own, att_other), pick(att_other, att_own)
        results[l] = (
            att_own[shard, :shard],
            att_a[:shard, :width],
            att_a[:shard, width:],
            att_b[:shard, width:],
            att_b[:shard, :width],
            att_own[shard + 1, :shard],
            pick(gate_up_own, gate_up_other),
            pick(gate_up_other, gate_up_own),
            jnp.concatenate([pick(down_own, down_other), pick(down_other, down_own)], axis=1),
        )
    stacked = [
        jnp.stack([results[l][m].astype(f32) for l in range(DECODER_LAYERS)], axis=0)
        for m in range(9)
    ]
    return (output, grad, *stacked)


def solution(mesh):
    weights = P(None, "fsdp", None)
    gains = P(None, "fsdp")
    packed = P(("rep", "fsdp"), None)
    in_specs = (
        packed,
        P("rep", None),
        gains,
        weights,
        weights,
        weights,
        weights,
        gains,
        weights,
        weights,
        weights,
        packed,
    )
    out_specs = (
        packed,
        packed,
        gains,
        weights,
        weights,
        weights,
        weights,
        gains,
        weights,
        weights,
        weights,
    )
    return jax.shard_map(body, mesh=mesh, in_specs=in_specs, out_specs=out_specs, check_vma=False)
```

```python
import functools

import jax
import jax.numpy as jnp
from jax import lax
from jax.experimental import pallas as pl
from jax.experimental.pallas import tpu as pltpu
from jax.sharding import PartitionSpec as P

QUERY_HEADS = 15
KEY_VALUE_HEADS = 5
GROUP = QUERY_HEADS // KEY_VALUE_HEADS
HEAD = 64
DECODER_LAYERS = 2
X_SIZE = 4

epsilon_norm = 1e-05
rope_base = 100000.0
masked_score = -1e30

f32 = jnp.float32
bf16 = jnp.bfloat16

NT = (((1,), (1,)), ((), ()))


def swap(array, axis, mask):
    count = lax.axis_size(axis)
    return lax.ppermute(array, axis, [(i, i ^ mask) for i in range(count)])


def swap_core(array):
    return swap(array, "rep", 1)


def gather_pack(rows):
    pair = jnp.stack([rows, swap(rows, "fsdp", 4)])
    parts = [pair] + [swap(pair, "fsdp", m) for m in range(1, X_SIZE)]
    return jnp.concatenate(parts, axis=0).reshape(-1, rows.shape[-1])


BLOCK_ORDER = (0, 4, 1, 5, 2, 6, 3, 7)


def scatter_pack(rows):
    blocks = rows.reshape(X_SIZE, 2, -1, rows.shape[-1])
    total = blocks[0].astype(f32)
    for m in range(1, X_SIZE):
        total = total + swap(blocks[m], "fsdp", m).astype(f32)
    return total[0] + swap(total[1].astype(bf16), "fsdp", 4).astype(f32)


def x_groups():
    return [[z * X_SIZE + x for x in range(X_SIZE)] for z in range(2)]


def sum_over_x(rows):
    return lax.psum_scatter(
        rows, "fsdp", scatter_dimension=0, tiled=True, axis_index_groups=x_groups()
    )


def to_owners(pair):
    z_hi = lax.axis_index("fsdp") // X_SIZE
    even = jnp.where(z_hi == 0, pair[0], pair[1])
    odd = jnp.where(z_hi == 0, pair[1], pair[0])
    reps, count = lax.axis_size("rep"), lax.axis_size("fsdp")

    def send(block, flip, z_lo):
        moves = []
        for rep in range(reps):
            for f in range(count):
                owner = 2 * (f % X_SIZE) + ((f // X_SIZE) ^ flip)
                moves.append((rep * count + f, (rep ^ (2 * z_lo)) * count + owner))
        return lax.ppermute(block, ("rep", "fsdp"), moves).astype(f32)

    near = send(even, 0, 0) + send(odd, 1, 0)
    far = send(even, 0, 1) + send(odd, 1, 1)
    return (near + far).astype(bf16)


def y_position():
    return lax.axis_index("rep") // 4


def sum_over_y(block_of):
    y = y_position()
    total = block_of(y).astype(f32)
    for m in range(1, 4):
        total = total + swap(block_of(jnp.bitwise_xor(y, m)), "rep", 4 * m).astype(f32)
    return total.astype(bf16)


def spread_over_y(block, axis):
    y = y_position()
    parts = [block] + [swap(block, "rep", 4 * m) for m in range(1, 4)]
    parts = [jnp.where(y % 2 == 1, parts[m ^ 1], parts[m]) for m in range(4)]
    parts = [jnp.where(y >= 2, parts[m ^ 2], parts[m]) for m in range(4)]
    return jnp.concatenate(parts, axis=axis)


def finish_rows(rows):
    count, columns = rows.shape
    blocks = rows.reshape(2, 4, count // 8, columns)
    total = sum_over_y(lambda k: lax.dynamic_index_in_dim(blocks, k, axis=1, keepdims=False))
    own = spread_over_y(to_owners(total), 0)
    return own, swap_core(own)


def finish_columns(columns):
    count, width = columns.shape
    own = spread_over_y(to_owners(columns.reshape(2, count // 2, width)), 1)
    return own, swap_core(own)


def kernel_params():
    return pltpu.CompilerParams(vmem_limit_bytes=48 * 1024 * 1024)


def assemble_kernel(count, y_parts, *refs):
    parts, out, sems = refs[:count], refs[count], refs[count + 1]
    me = lax.axis_index("fsdp")
    copies = []
    if y_parts:
        y = lax.axis_index("rep") // 4
        columns = parts[0].shape[-1]
        for m in range(count):
            first = pl.multiple_of(jnp.bitwise_xor(y, m) * columns, 128)
            for k, block in enumerate(BLOCK_ORDER):
                place = out.at[jnp.bitwise_xor(me, block), :, pl.ds(first, columns)]
                copies.append((parts[m].at[k], place))
    else:
        for k, block in enumerate(BLOCK_ORDER):
            copies.append((parts[k // 2].at[k % 2], out.at[jnp.bitwise_xor(me, block)]))
    copies = [
        pltpu.make_async_copy(source, place, sems.at[i])
        for i, (source, place) in enumerate(copies)
    ]
    for copy in copies:
        copy.start()
    for copy in copies:
        copy.wait()


def assemble(parts, y_parts):
    rows, columns = parts[0].shape[1:]
    blocks = len(BLOCK_ORDER)
    columns = columns * len(parts) if y_parts else columns
    size = blocks * rows * columns * 4
    return pl.pallas_call(
        functools.partial(assemble_kernel, len(parts), y_parts),
        out_shape=jax.ShapeDtypeStruct((blocks, rows, columns), parts[0].dtype),
        in_specs=[pl.BlockSpec(memory_space=pl.ANY)] * len(parts),
        out_specs=pl.BlockSpec(memory_space=pltpu.VMEM),
        compiler_params=kernel_params(),
        scratch_shapes=[pltpu.SemaphoreType.DMA((blocks * (len(parts) if y_parts else 1),))],
        cost_estimate=pl.CostEstimate(flops=0, bytes_accessed=size, transcendentals=0),
        name="assemble",
    )(*parts)


def after(array, earlier):
    return lax.optimization_barrier((array, earlier))[0]


def gather_blocks(part, earlier):
    pair = jnp.stack([part, swap(part, "fsdp", 4)])
    pair = pair if earlier is None else after(pair, earlier)
    return [pair] + [swap(pair, "fsdp", m) for m in range(1, X_SIZE)]


def gather_by_y(part, earlier):
    columns = part.shape[1] // 4
    y = y_position()
    quarter = lax.dynamic_slice_in_dim(part, y * columns, columns, axis=1)
    blocks = gather_blocks(quarter, earlier)
    joined = jnp.concatenate(blocks, axis=0)
    parts = [joined] + [swap(joined, "rep", 4 * m) for m in range(1, 4)]
    return parts, blocks


def stacked_heads(array, kv_head):
    first = kv_head * GROUP
    return jnp.concatenate(
        [array[:, (first + g) * HEAD : (first + g + 1) * HEAD] for g in range(GROUP)], axis=0
    )


def attention_forward_kernel(q_ref, kv_ref, key_place_ref, bounds_ref, mixed_ref, log_ref, bias):
    rows = q_ref.shape[0]
    keys = kv_ref.shape[0]
    width = KEY_VALUE_HEADS * HEAD
    place = key_place_ref[...]
    bias[...] = jnp.where(
        (place >= bounds_ref[0:1, :]) & (place <= bounds_ref[1:2, :]), 0.0, masked_score
    )
    for h in range(KEY_VALUE_HEADS):
        queries = stacked_heads(q_ref[...], h)
        keys_h = kv_ref[:, h * HEAD : (h + 1) * HEAD]
        values_h = kv_ref[:, width + h * HEAD : width + (h + 1) * HEAD]
        scores = lax.dot_general(keys_h, queries, NT, preferred_element_type=f32) + bias[...]
        top = jnp.max(scores, axis=0, keepdims=True)
        weights = jnp.exp(scores - top)
        total = jnp.sum(weights, axis=0, keepdims=True)
        mixed = jnp.dot(
            values_h.T, weights.astype(bf16), preferred_element_type=f32
        ) * (1.0 / total)
        mixed = mixed.T.astype(bf16)
        for g in range(GROUP):
            j = h * GROUP + g
            mixed_ref[:, j * HEAD : (j + 1) * HEAD] = mixed[g * rows : (g + 1) * rows]
        log_ref[h : h + 1, :] = top + jnp.log(total)


def attention_backward_kernel(
    q_ref, kv_ref, key_place_ref, bounds_ref, mixed_ref, log_ref, grad_ref, dq_ref, dkv_ref
):
    rows = q_ref.shape[0]
    keys = kv_ref.shape[0]
    width = KEY_VALUE_HEADS * HEAD
    chunk = keys // 4
    for h in range(KEY_VALUE_HEADS):
        queries = stacked_heads(q_ref[...], h)
        grads = stacked_heads(grad_ref[...], h)
        mixed = stacked_heads(mixed_ref[...], h)
        product = (grads.astype(f32) * mixed.astype(f32)).T
        delta = jnp.sum(product, axis=0, keepdims=True)
        logs = log_ref[h : h + 1, :]
        dq = jnp.zeros((HEAD, GROUP * rows), f32)
        for part in range(4):
            span = slice(part * chunk, (part + 1) * chunk)
            place = key_place_ref[span, :]
            allowed = (place >= bounds_ref[0:1, :]) & (place <= bounds_ref[1:2, :])
            keys_h = kv_ref[span, h * HEAD : (h + 1) * HEAD]
            values_h = kv_ref[span, width + h * HEAD : width + (h + 1) * HEAD]
            scores = lax.dot_general(keys_h, queries, NT, preferred_element_type=f32)
            weights = jnp.exp(jnp.where(allowed, scores, masked_score) - logs)
            dweights = lax.dot_general(values_h, grads, NT, preferred_element_type=f32)
            dscores = (weights * (dweights - delta)).astype(bf16)
            dvalues = jnp.dot(weights.astype(bf16), grads, preferred_element_type=f32)
            dkeys = jnp.dot(dscores, queries, preferred_element_type=f32)
            dq = dq + jnp.dot(keys_h.T, dscores, preferred_element_type=f32)
            dkv_ref[span, h * HEAD : (h + 1) * HEAD] = dkeys.astype(bf16)
            dkv_ref[span, width + h * HEAD : width + (h + 1) * HEAD] = dvalues.astype(bf16)
        dq = dq.T * HEAD ** (-0.5)
        for g in range(GROUP):
            j = h * GROUP + g
            dq_ref[:, j * HEAD : (j + 1) * HEAD] = dq[g * rows : (g + 1) * rows]


def attend(queries, kv, key_place, bounds):
    rows, keys = queries.shape[0], kv.shape[0]
    pairs = QUERY_HEADS * rows * keys
    return pl.pallas_call(
        attention_forward_kernel,
        out_shape=(
            jax.ShapeDtypeStruct(queries.shape, bf16),
            jax.ShapeDtypeStruct((8, GROUP * rows), f32),
        ),
        scratch_shapes=[pltpu.VMEM((keys, GROUP * rows), f32)],
        compiler_params=kernel_params(),
        cost_estimate=pl.CostEstimate(
            flops=4 * pairs * HEAD, bytes_accessed=4 * 1024 * 1024, transcendentals=pairs
        ),
        name="attention_forward",
    )(queries, kv, key_place, bounds)


def attend_back(queries, kv, key_place, bounds, mixed, logs, grads):
    rows, keys = queries.shape[0], kv.shape[0]
    pairs = QUERY_HEADS * rows * keys
    return pl.pallas_call(
        attention_backward_kernel,
        out_shape=(
            jax.ShapeDtypeStruct(queries.shape, f32),
            jax.ShapeDtypeStruct(kv.shape, bf16),
        ),
        compiler_params=kernel_params(),
        cost_estimate=pl.CostEstimate(
            flops=10 * pairs * HEAD, bytes_accessed=6 * 1024 * 1024, transcendentals=pairs
        ),
        name="attention_backward",
    )(queries, kv, key_place, bounds, mixed, logs, grads)


def normalize(stream):
    return stream * lax.rsqrt(jnp.mean(stream * stream, axis=-1, keepdims=True) + epsilon_norm)


def normalize_back(stream, gain, grad):
    inverse = lax.rsqrt(jnp.mean(stream * stream, axis=-1, keepdims=True) + epsilon_norm)
    unit = stream * inverse
    scaled = grad * gain
    gain_grad = jnp.sum(grad * unit, axis=0)
    return inverse * (scaled - unit * jnp.mean(scaled * unit, axis=-1, keepdims=True)), gain_grad


def turn(flat):
    half = HEAD // 2
    ahead = jnp.concatenate([flat[:, half:], flat[:, :half]], axis=1)
    behind = jnp.concatenate([flat[:, -half:], flat[:, :-half]], axis=1)
    lane = lax.broadcasted_iota(jnp.int32, flat.shape, 1) % HEAD
    return jnp.where(lane < half, -ahead, behind)


def rotary(flat, cosine, sine):
    return flat * cosine[:, : flat.shape[1]] + turn(flat) * sine[:, : flat.shape[1]]


def rotary_back(flat, cosine, sine):
    return flat * cosine[:, : flat.shape[1]] - turn(flat * sine[:, : flat.shape[1]])


def matmul(left, right):
    return jnp.dot(left, right, preferred_element_type=f32)


def matmul_nt(left, right):
    return lax.dot_general(left, right, NT, preferred_element_type=f32)


def cross_rows(left, right):
    return lax.dot_general(left, right, (((0,), (0,)), ((), ())), preferred_element_type=f32)


def body(
    tokens,
    seq_lengths,
    attn_gain,
    query_weight,
    key_projection,
    value_projection,
    out_weight,
    mlp_gain,
    gate_weight,
    up_weight,
    down_weight,
    cotangent,
):
    rows, width = tokens.shape
    shard = query_weight.shape[1]
    key_width = key_projection.shape[2]
    att_width = width + key_width
    half_width = width // 2
    me = lax.axis_index("fsdp")
    first_core = lax.axis_index("rep") % 2 == 0

    def pick(a, b):
        return jnp.where(first_core, a, b)

    lengths = seq_lengths[0]
    ends = jnp.cumsum(lengths)
    starts = ends - lengths
    places = me * rows + jnp.arange(rows, dtype=jnp.int32)
    segment = jnp.sum((places[:, None] >= ends[None, :-1]).astype(jnp.int32), axis=1)
    chosen = segment[:, None] == jnp.arange(lengths.shape[0], dtype=jnp.int32)[None, :]
    start = jnp.sum(chosen.astype(jnp.int32) * starts[None, :], axis=1)
    offsets = (places - start).astype(f32)
    frequency = rope_base ** (-(jnp.arange(HEAD // 2, dtype=f32) * 2.0) / HEAD)
    angles = offsets[:, None] * frequency[None, :]
    cosine = jnp.tile(jnp.cos(angles), (1, 2 * QUERY_HEADS))
    sine = jnp.tile(jnp.sin(angles), (1, 2 * QUERY_HEADS))
    bounds = jnp.stack([jnp.tile(start, GROUP), jnp.tile(places, GROUP)])
    bounds = jnp.pad(bounds, ((0, 6), (0, 0)))
    blocks = jnp.bitwise_xor(me, jnp.array(BLOCK_ORDER, jnp.int32))
    key_place = blocks[:, None] * rows + jnp.arange(rows, dtype=jnp.int32)[None, :]
    key_place = key_place.reshape(-1, 1)

    def own_weights(l):
        gains = jnp.stack([attn_gain[l], mlp_gain[l]])
        gains = jnp.pad(gains, ((0, 6), (0, att_width - shard)))
        att = pick(
            jnp.concatenate([query_weight[l], key_projection[l]], axis=1),
            jnp.concatenate([out_weight[l], value_projection[l]], axis=1),
        )
        att = jnp.concatenate([att, gains], axis=0)
        gate_up = pick(gate_weight[l], up_weight[l])
        down = pick(down_weight[l][:, :half_width], down_weight[l][:, half_width:])
        return att, gate_up, down

    def gather_parts(own):
        att, gate_up, down = own
        by_y, _ = gather_by_y(gate_up, None)
        att_parts = gather_blocks(att, None)
        return att_parts, by_y, gather_blocks(down, att_parts)

    def attention_weights(att_parts):
        mine = assemble(att_parts, False)
        other = swap_core(mine)
        gain_attn = mine[:, shard, :shard].reshape(width).astype(f32)
        gain_mlp = mine[:, shard + 1, :shard].reshape(width).astype(f32)
        mine = mine[:, :shard].reshape(width, att_width)
        other = other[:, :shard].reshape(width, att_width)
        return gain_attn, gain_mlp, pick(mine, other), pick(other, mine)

    def mlp_weights(by_y, down_parts):
        mine = assemble(by_y, True).reshape(width, -1)
        gate_up = (mine, swap_core(mine))
        mine = assemble(down_parts, False).reshape(-1, half_width)
        return gate_up, (mine, swap_core(mine))

    stream = tokens.astype(f32)
    saved = []
    layers = []
    parts = gather_parts(own_weights(0))
    for l in range(DECODER_LAYERS):
        att_parts, by_y, down_parts = parts
        gain_attn, gain_mlp, query_key, out_value = attention_weights(att_parts)
        normed = (normalize(stream) * gain_attn).astype(bf16)
        values = matmul(normed, out_value[:, width:]).astype(bf16)
        projected = matmul(normed, query_key)
        keys = rotary(projected[:, width:], cosine, sine).astype(bf16)
        kv = gather_pack(jnp.concatenate([keys, values], axis=1))
        if l + 1 < DECODER_LAYERS:
            parts = gather_parts(after(own_weights(l + 1), kv))
        queries = rotary(projected[:, :width], cosine, sine).astype(bf16)
        queries = queries * jnp.asarray(HEAD ** (-0.5), bf16)
        mixed, logs = attend(queries, kv, key_place, bounds)
        gate_up, down = mlp_weights(*after((by_y, down_parts), mixed))
        layers.append((gain_attn, gain_mlp, query_key, out_value, gate_up, down))
        middle = stream + matmul(mixed, out_value[:, :width])
        normed_mlp = (normalize(middle) * gain_mlp).astype(bf16)
        mine = matmul(normed_mlp, gate_up[0])
        other = matmul(normed_mlp, gate_up[1])
        gate, up = pick(mine, other), pick(other, mine)
        sigmoid = jax.nn.sigmoid(gate)
        hidden = (gate * sigmoid * up).astype(bf16)
        mine = matmul(hidden, down[0])
        other = matmul(hidden, down[1])
        saved.append((stream, normed, queries, kv, logs, mixed, middle, normed_mlp, gate, up, hidden))
        stream = middle + jnp.concatenate([pick(mine, other), pick(other, mine)], axis=1)
    output = stream.astype(bf16)

    sums = ()
    mlp_done = att_done = ()
    grad = cotangent.astype(f32)
    results = [None] * DECODER_LAYERS
    for l in reversed(range(DECODER_LAYERS)):
        gain_attn, gain_mlp, query_key, out_value, gate_up, down = layers[l]
        stream, normed, queries, kv, logs, mixed, middle, normed_mlp, gate, up, hidden = saved[l]
        grad_low = grad.astype(bf16)
        grad_a, grad_b = grad_low[:, :half_width], grad_low[:, half_width:]
        grad_mine, grad_other = pick(grad_a, grad_b), pick(grad_b, grad_a)
        down_received = swap_core(cross_rows(hidden, grad_other).astype(bf16))
        down_sum = (cross_rows(hidden, grad_mine) + down_received.astype(f32)).astype(bf16)
        down_sum = sum_over_x(after(down_sum, sums))

        dhidden = matmul_nt(grad_mine, down[0]) + matmul_nt(grad_other, down[1])
        sigmoid = jax.nn.sigmoid(gate)
        dgate = (dhidden * up * sigmoid * (1.0 + gate * (1.0 - sigmoid))).astype(bf16)
        dup = (dhidden * gate * sigmoid).astype(bf16)
        dmine, dother = pick(dgate, dup), pick(dup, dgate)
        gate_up_received = swap_core(cross_rows(normed_mlp, dother).astype(bf16))
        gate_up_sum = cross_rows(normed_mlp, dmine) + gate_up_received.astype(f32)
        gate_up_sum = gate_up_sum.astype(bf16)
        columns = gate_up_sum.shape[1] // 4
        gate_up_sum = sum_over_y(
            lambda k: lax.dynamic_slice_in_dim(gate_up_sum, k * columns, columns, axis=1)
        )
        gate_up_sum = sum_over_x(after(gate_up_sum, sums))

        dnormed = matmul_nt(dmine, gate_up[0]) + matmul_nt(dother, gate_up[1])
        dmiddle, mlp_gain_grad = normalize_back(middle, gain_mlp, dnormed)
        dmiddle = dmiddle + grad
        dmiddle_low = dmiddle.astype(bf16)
        dmixed = matmul_nt(dmiddle_low, out_value[:, :width]).astype(bf16)
        dmixed = after(dmixed, mlp_done)
        dq, dkv = attend_back(queries, kv, key_place, bounds, mixed, logs, dmixed)
        dkv = after(dkv, (down_received, gate_up_received))
        dkv = after(scatter_pack(dkv), att_done)
        dq = rotary_back(dq, cosine, sine).astype(bf16)
        dk = rotary_back(dkv[:, :key_width], cosine, sine).astype(bf16)
        dv = dkv[:, key_width:].astype(bf16)

        dqk = jnp.concatenate([dq, dk], axis=1)
        dnormed = matmul_nt(dqk, query_key) + matmul_nt(dv, out_value[:, width:])
        dstream, attn_gain_grad = normalize_back(stream, gain_attn, dnormed)
        grad = dstream + dmiddle

        def att_terms(first):
            wide = cross_rows(
                jnp.where(first, normed, mixed), jnp.where(first, dq, dmiddle_low)
            )
            return jnp.concatenate([wide, cross_rows(normed, jnp.where(first, dk, dv))], axis=1)

        received = swap_core(att_terms(jnp.logical_not(first_core)).astype(bf16))
        att_sum = (att_terms(first_core) + received.astype(f32)).astype(bf16)
        gain_grads = jnp.stack([attn_gain_grad, mlp_gain_grad]).astype(bf16)
        received = swap_core(gain_grads)
        gain_grads = (gain_grads.astype(f32) + received.astype(f32)).astype(bf16)
        gain_grads = gain_grads.reshape(2, -1, shard).swapaxes(0, 1)
        gain_grads = jnp.pad(gain_grads, ((0, 0), (0, 6), (0, att_width - shard)))
        att_sum = jnp.concatenate([att_sum.reshape(-1, shard, att_width), gain_grads], axis=1)
        att_sum = sum_over_x(att_sum.reshape(-1, att_width))
        sums = (down_sum, gate_up_sum, att_sum)

        mlp_done = (*finish_columns(gate_up_sum), *finish_rows(down_sum))
        gate_up_own, gate_up_other, down_own, down_other = mlp_done
        att_done = finish_rows(att_sum)
        att_own, att_other = att_done
        att_a, att_b = pick(att_own, att_other), pick(att_other, att_own)
        results[l] = (
            att_own[shard, :shard],
            att_a[:shard, :width],
            att_a[:shard, width:],
            att_b[:shard, width:],
            att_b[:shard, :width],
            att_own[shard + 1, :shard],
            pick(gate_up_own, gate_up_other),
            pick(gate_up_other, gate_up_own),
            jnp.concatenate([pick(down_own, down_other), pick(down_other, down_own)], axis=1),
        )
    stacked = [
        jnp.stack([results[l][m].astype(f32) for l in range(DECODER_LAYERS)], axis=0)
        for m in range(9)
    ]
    return (output, grad, *stacked)


def solution(mesh):
    weights = P(None, "fsdp", None)
    gains = P(None, "fsdp")
    packed = P(("rep", "fsdp"), None)
    in_specs = (
        packed,
        P("rep", None),
        gains,
        weights,
        weights,
        weights,
        weights,
        gains,
        weights,
        weights,
        weights,
        packed,
    )
    out_specs = (
        packed,
        packed,
        gains,
        weights,
        weights,
        weights,
        weights,
        gains,
        weights,
        weights,
        weights,
    )
    return jax.shard_map(body, mesh=mesh, in_specs=in_specs, out_specs=out_specs, check_vma=False)
```

```python
import functools

import jax
import jax.numpy as jnp
from jax import lax
from jax.experimental import pallas as pl
from jax.experimental.pallas import tpu as pltpu
from jax.sharding import PartitionSpec as P

QUERY_HEADS = 15
KEY_VALUE_HEADS = 5
GROUP = QUERY_HEADS // KEY_VALUE_HEADS
HEAD = 64
DECODER_LAYERS = 2
X_SIZE = 4

epsilon_norm = 1e-05
rope_base = 100000.0
masked_score = -1e30

f32 = jnp.float32
bf16 = jnp.bfloat16

NT = (((1,), (1,)), ((), ()))


def swap(array, axis, mask):
    count = lax.axis_size(axis)
    return lax.ppermute(array, axis, [(i, i ^ mask) for i in range(count)])


def swap_core(array):
    return swap(array, "rep", 1)


def gather_pack(rows):
    pair = jnp.stack([rows, swap(rows, "fsdp", 4)])
    parts = [pair] + [swap(pair, "fsdp", m) for m in range(1, X_SIZE)]
    return jnp.concatenate(parts, axis=0).reshape(-1, rows.shape[-1])


BLOCK_ORDER = (0, 4, 1, 5, 2, 6, 3, 7)


def scatter_pack(rows):
    blocks = rows.reshape(X_SIZE, 2, -1, rows.shape[-1])
    total = blocks[0].astype(f32)
    for m in range(1, X_SIZE):
        total = total + swap(blocks[m], "fsdp", m).astype(f32)
    return total[0] + swap(total[1].astype(bf16), "fsdp", 4).astype(f32)


def x_groups():
    return [[z * X_SIZE + x for x in range(X_SIZE)] for z in range(2)]


def sum_over_x(rows):
    return lax.psum_scatter(
        rows, "fsdp", scatter_dimension=0, tiled=True, axis_index_groups=x_groups()
    )


def to_owners(pair):
    z_hi = lax.axis_index("fsdp") // X_SIZE
    even = jnp.where(z_hi == 0, pair[0], pair[1])
    odd = jnp.where(z_hi == 0, pair[1], pair[0])
    reps, count = lax.axis_size("rep"), lax.axis_size("fsdp")

    def send(block, flip, z_lo):
        moves = []
        for rep in range(reps):
            for f in range(count):
                owner = 2 * (f % X_SIZE) + ((f // X_SIZE) ^ flip)
                moves.append((rep * count + f, (rep ^ (2 * z_lo)) * count + owner))
        return lax.ppermute(block, ("rep", "fsdp"), moves).astype(f32)

    near = send(even, 0, 0) + send(odd, 1, 0)
    far = send(even, 0, 1) + send(odd, 1, 1)
    return (near + far).astype(bf16)


def y_position():
    return lax.axis_index("rep") // 4


def sum_over_y(block_of):
    y = y_position()
    total = block_of(y).astype(f32)
    for m in range(1, 4):
        total = total + swap(block_of(jnp.bitwise_xor(y, m)), "rep", 4 * m).astype(f32)
    return total.astype(bf16)


def spread_over_y(block, axis):
    y = y_position()
    parts = [block] + [swap(block, "rep", 4 * m) for m in range(1, 4)]
    parts = [jnp.where(y % 2 == 1, parts[m ^ 1], parts[m]) for m in range(4)]
    parts = [jnp.where(y >= 2, parts[m ^ 2], parts[m]) for m in range(4)]
    return jnp.concatenate(parts, axis=axis)


LAST = 640


def as_rows(array):
    columns = array.shape[2]
    parts = []
    for first in range(0, columns, LAST):
        part = array[:, :, first : first + LAST]
        parts.append(jnp.pad(part, ((0, 0), (0, 0), (0, LAST - part.shape[2]))))
    return jnp.concatenate(parts, axis=1)


def finish_sums(summed, quarter):
    joined = jnp.concatenate([as_rows(array) for array in summed], axis=1)
    height = joined.shape[1] // 4
    blocks = joined.reshape(2, 4, height, LAST)
    total = sum_over_y(lambda k: lax.dynamic_index_in_dim(blocks, k, axis=1, keepdims=False))
    if quarter is not None:
        total = jnp.concatenate([total, quarter], axis=1)
    own = spread_over_y(to_owners(total)[None], 0)

    def take_apart(spread):
        rows = spread[:, :height].reshape(4 * height, LAST)
        results, first = [], 0
        for array in summed:
            count, columns = array.shape[1:]
            parts = []
            for start in range(0, columns, LAST):
                parts.append(rows[first : first + count, : min(LAST, columns - start)])
                first += count
            results.append(jnp.concatenate(parts, axis=1))
        if quarter is not None:
            results.append(jnp.concatenate([spread[k, height:] for k in range(4)], axis=1))
        return results

    return take_apart(own), take_apart(swap_core(own))


def kernel_params():
    return pltpu.CompilerParams(vmem_limit_bytes=48 * 1024 * 1024)


def assemble_kernel(count, y_parts, *refs):
    parts, out, sems = refs[:count], refs[count], refs[count + 1]
    me = lax.axis_index("fsdp")
    copies = []
    if y_parts:
        y = lax.axis_index("rep") // 4
        columns = parts[0].shape[-1]
        for m in range(count):
            first = pl.multiple_of(jnp.bitwise_xor(y, m) * columns, 128)
            for k, block in enumerate(BLOCK_ORDER):
                place = out.at[jnp.bitwise_xor(me, block), :, pl.ds(first, columns)]
                copies.append((parts[m].at[k], place))
    else:
        for k, block in enumerate(BLOCK_ORDER):
            copies.append((parts[k // 2].at[k % 2], out.at[jnp.bitwise_xor(me, block)]))
    copies = [
        pltpu.make_async_copy(source, place, sems.at[i])
        for i, (source, place) in enumerate(copies)
    ]
    for copy in copies:
        copy.start()
    for copy in copies:
        copy.wait()


def assemble(parts, y_parts):
    rows, columns = parts[0].shape[1:]
    blocks = len(BLOCK_ORDER)
    columns = columns * len(parts) if y_parts else columns
    size = blocks * rows * columns * 4
    return pl.pallas_call(
        functools.partial(assemble_kernel, len(parts), y_parts),
        out_shape=jax.ShapeDtypeStruct((blocks, rows, columns), parts[0].dtype),
        in_specs=[pl.BlockSpec(memory_space=pl.ANY)] * len(parts),
        out_specs=pl.BlockSpec(memory_space=pltpu.VMEM),
        compiler_params=kernel_params(),
        scratch_shapes=[pltpu.SemaphoreType.DMA((blocks * (len(parts) if y_parts else 1),))],
        cost_estimate=pl.CostEstimate(flops=0, bytes_accessed=size, transcendentals=0),
        name="assemble",
    )(*parts)


def after(array, earlier):
    return lax.optimization_barrier((array, earlier))[0]


def gather_blocks(part, earlier):
    pair = jnp.stack([part, swap(part, "fsdp", 4)])
    pair = pair if earlier is None else after(pair, earlier)
    return [pair] + [swap(pair, "fsdp", m) for m in range(1, X_SIZE)]


def gather_by_y(part, earlier):
    columns = part.shape[1] // 4
    y = y_position()
    quarter = lax.dynamic_slice_in_dim(part, y * columns, columns, axis=1)
    blocks = gather_blocks(quarter, earlier)
    joined = jnp.concatenate(blocks, axis=0)
    parts = [joined] + [swap(joined, "rep", 4 * m) for m in range(1, 4)]
    return parts, joined


def stacked_heads(array, kv_head):
    first = kv_head * GROUP
    return jnp.concatenate(
        [array[:, (first + g) * HEAD : (first + g + 1) * HEAD] for g in range(GROUP)], axis=0
    )


def attention_forward_kernel(q_ref, kv_ref, key_place_ref, bounds_ref, mixed_ref, log_ref, bias):
    rows = q_ref.shape[0]
    keys = kv_ref.shape[0]
    width = KEY_VALUE_HEADS * HEAD
    place = key_place_ref[...]
    bias[...] = jnp.where(
        (place >= bounds_ref[0:1, :]) & (place <= bounds_ref[1:2, :]), 0.0, masked_score
    )
    for h in range(KEY_VALUE_HEADS):
        queries = stacked_heads(q_ref[...], h)
        keys_h = kv_ref[:, h * HEAD : (h + 1) * HEAD]
        values_h = kv_ref[:, width + h * HEAD : width + (h + 1) * HEAD]
        scores = lax.dot_general(keys_h, queries, NT, preferred_element_type=f32) + bias[...]
        top = jnp.max(scores, axis=0, keepdims=True)
        weights = jnp.exp(scores - top)
        total = jnp.sum(weights, axis=0, keepdims=True)
        mixed = jnp.dot(
            values_h.T, weights.astype(bf16), preferred_element_type=f32
        ) * (1.0 / total)
        mixed = mixed.T.astype(bf16)
        for g in range(GROUP):
            j = h * GROUP + g
            mixed_ref[:, j * HEAD : (j + 1) * HEAD] = mixed[g * rows : (g + 1) * rows]
        log_ref[h : h + 1, :] = top + jnp.log(total)


def attention_backward_kernel(
    q_ref, kv_ref, key_place_ref, bounds_ref, mixed_ref, log_ref, grad_ref, dq_ref, dkv_ref
):
    rows = q_ref.shape[0]
    keys = kv_ref.shape[0]
    width = KEY_VALUE_HEADS * HEAD
    chunk = keys // 4
    for h in range(KEY_VALUE_HEADS):
        queries = stacked_heads(q_ref[...], h)
        grads = stacked_heads(grad_ref[...], h)
        mixed = stacked_heads(mixed_ref[...], h)
        product = (grads.astype(f32) * mixed.astype(f32)).T
        delta = jnp.sum(product, axis=0, keepdims=True)
        logs = log_ref[h : h + 1, :]
        dq = jnp.zeros((HEAD, GROUP * rows), f32)
        for part in range(4):
            span = slice(part * chunk, (part + 1) * chunk)
            place = key_place_ref[span, :]
            allowed = (place >= bounds_ref[0:1, :]) & (place <= bounds_ref[1:2, :])
            keys_h = kv_ref[span, h * HEAD : (h + 1) * HEAD]
            values_h = kv_ref[span, width + h * HEAD : width + (h + 1) * HEAD]
            scores = lax.dot_general(keys_h, queries, NT, preferred_element_type=f32)
            weights = jnp.exp(jnp.where(allowed, scores, masked_score) - logs)
            dweights = lax.dot_general(values_h, grads, NT, preferred_element_type=f32)
            dscores = (weights * (dweights - delta)).astype(bf16)
            dvalues = jnp.dot(weights.astype(bf16), grads, preferred_element_type=f32)
            dkeys = jnp.dot(dscores, queries, preferred_element_type=f32)
            dq = dq + jnp.dot(keys_h.T, dscores, preferred_element_type=f32)
            dkv_ref[span, h * HEAD : (h + 1) * HEAD] = dkeys.astype(bf16)
            dkv_ref[span, width + h * HEAD : width + (h + 1) * HEAD] = dvalues.astype(bf16)
        dq = dq.T * HEAD ** (-0.5)
        for g in range(GROUP):
            j = h * GROUP + g
            dq_ref[:, j * HEAD : (j + 1) * HEAD] = dq[g * rows : (g + 1) * rows]


def attend(queries, kv, key_place, bounds):
    rows, keys = queries.shape[0], kv.shape[0]
    pairs = QUERY_HEADS * rows * keys
    return pl.pallas_call(
        attention_forward_kernel,
        out_shape=(
            jax.ShapeDtypeStruct(queries.shape, bf16),
            jax.ShapeDtypeStruct((8, GROUP * rows), f32),
        ),
        scratch_shapes=[pltpu.VMEM((keys, GROUP * rows), f32)],
        compiler_params=kernel_params(),
        cost_estimate=pl.CostEstimate(
            flops=4 * pairs * HEAD, bytes_accessed=4 * 1024 * 1024, transcendentals=pairs
        ),
        name="attention_forward",
    )(queries, kv, key_place, bounds)


def attend_back(queries, kv, key_place, bounds, mixed, logs, grads):
    rows, keys = queries.shape[0], kv.shape[0]
    pairs = QUERY_HEADS * rows * keys
    return pl.pallas_call(
        attention_backward_kernel,
        out_shape=(
            jax.ShapeDtypeStruct(queries.shape, f32),
            jax.ShapeDtypeStruct(kv.shape, bf16),
        ),
        compiler_params=kernel_params(),
        cost_estimate=pl.CostEstimate(
            flops=10 * pairs * HEAD, bytes_accessed=6 * 1024 * 1024, transcendentals=pairs
        ),
        name="attention_backward",
    )(queries, kv, key_place, bounds, mixed, logs, grads)


def normalize(stream):
    return stream * lax.rsqrt(jnp.mean(stream * stream, axis=-1, keepdims=True) + epsilon_norm)


def normalize_back(stream, gain, grad):
    inverse = lax.rsqrt(jnp.mean(stream * stream, axis=-1, keepdims=True) + epsilon_norm)
    unit = stream * inverse
    scaled = grad * gain
    gain_grad = jnp.sum(grad * unit, axis=0)
    return inverse * (scaled - unit * jnp.mean(scaled * unit, axis=-1, keepdims=True)), gain_grad


def turn(flat):
    half = HEAD // 2
    ahead = jnp.concatenate([flat[:, half:], flat[:, :half]], axis=1)
    behind = jnp.concatenate([flat[:, -half:], flat[:, :-half]], axis=1)
    lane = lax.broadcasted_iota(jnp.int32, flat.shape, 1) % HEAD
    return jnp.where(lane < half, -ahead, behind)


def rotary(flat, cosine, sine):
    return flat * cosine[:, : flat.shape[1]] + turn(flat) * sine[:, : flat.shape[1]]


def rotary_back(flat, cosine, sine):
    return flat * cosine[:, : flat.shape[1]] - turn(flat * sine[:, : flat.shape[1]])


def matmul(left, right):
    return jnp.dot(left, right, preferred_element_type=f32)


def matmul_nt(left, right):
    return lax.dot_general(left, right, NT, preferred_element_type=f32)


def cross_rows(left, right):
    return lax.dot_general(left, right, (((0,), (0,)), ((), ())), preferred_element_type=f32)


def body(
    tokens,
    seq_lengths,
    attn_gain,
    query_weight,
    key_projection,
    value_projection,
    out_weight,
    mlp_gain,
    gate_weight,
    up_weight,
    down_weight,
    cotangent,
):
    rows, width = tokens.shape
    shard = query_weight.shape[1]
    key_width = key_projection.shape[2]
    att_width = width + key_width
    half_width = width // 2
    me = lax.axis_index("fsdp")
    first_core = lax.axis_index("rep") % 2 == 0

    def pick(a, b):
        return jnp.where(first_core, a, b)

    lengths = seq_lengths[0]
    ends = jnp.cumsum(lengths)
    starts = ends - lengths
    places = me * rows + jnp.arange(rows, dtype=jnp.int32)
    segment = jnp.sum((places[:, None] >= ends[None, :-1]).astype(jnp.int32), axis=1)
    chosen = segment[:, None] == jnp.arange(lengths.shape[0], dtype=jnp.int32)[None, :]
    start = jnp.sum(chosen.astype(jnp.int32) * starts[None, :], axis=1)
    offsets = (places - start).astype(f32)
    frequency = rope_base ** (-(jnp.arange(HEAD // 2, dtype=f32) * 2.0) / HEAD)
    angles = offsets[:, None] * frequency[None, :]
    cosine = jnp.tile(jnp.cos(angles), (1, 2 * QUERY_HEADS))
    sine = jnp.tile(jnp.sin(angles), (1, 2 * QUERY_HEADS))
    bounds = jnp.stack([jnp.tile(start, GROUP), jnp.tile(places, GROUP)])
    bounds = jnp.pad(bounds, ((0, 6), (0, 0)))
    blocks = jnp.bitwise_xor(me, jnp.array(BLOCK_ORDER, jnp.int32))
    key_place = blocks[:, None] * rows + jnp.arange(rows, dtype=jnp.int32)[None, :]
    key_place = key_place.reshape(-1, 1)

    def own_weights(l):
        gains = jnp.stack([attn_gain[l], mlp_gain[l]])
        gains = jnp.pad(gains, ((0, 6), (0, att_width - shard)))
        att = pick(
            jnp.concatenate([query_weight[l], key_projection[l]], axis=1),
            jnp.concatenate([out_weight[l], value_projection[l]], axis=1),
        )
        att = jnp.concatenate([att, gains], axis=0)
        gate_up = pick(gate_weight[l], up_weight[l])
        down = pick(down_weight[l][:, :half_width], down_weight[l][:, half_width:])
        return att, gate_up, down

    def gather_parts(own):
        att, gate_up, down = own
        att_parts = gather_blocks(att, None)
        by_y, by_x = gather_by_y(gate_up, None)
        return att_parts, by_y, by_x, down

    def attention_weights(att_parts):
        mine = assemble(att_parts, False)
        other = swap_core(mine)
        gain_attn = mine[:, shard, :shard].reshape(width).astype(f32)
        gain_mlp = mine[:, shard + 1, :shard].reshape(width).astype(f32)
        mine = mine[:, :shard].reshape(width, att_width)
        other = other[:, :shard].reshape(width, att_width)
        return gain_attn, gain_mlp, pick(mine, other), pick(other, mine)

    def mlp_weights(by_y, down_parts):
        mine = assemble(by_y, True).reshape(width, -1)
        gate_up = (mine, swap_core(mine))
        mine = assemble(down_parts, False).reshape(-1, half_width)
        return gate_up, (mine, swap_core(mine))

    stream = tokens.astype(f32)
    saved = []
    layers = []
    parts = gather_parts(own_weights(0))
    for l in range(DECODER_LAYERS):
        att_parts, by_y, by_x, own_down = parts
        att_parts = after(att_parts, stream)
        gain_attn, gain_mlp, query_key, out_value = attention_weights(att_parts)
        normed = (normalize(stream) * gain_attn).astype(bf16)
        values = matmul(normed, out_value[:, width:]).astype(bf16)
        projected = matmul(normed, query_key)
        keys = rotary(projected[:, width:], cosine, sine).astype(bf16)
        kv = gather_pack(after(jnp.concatenate([keys, values], axis=1), by_x))
        down_parts = gather_blocks(own_down, kv)
        if l + 1 < DECODER_LAYERS:
            parts = gather_parts(after(own_weights(l + 1), kv))
        queries = rotary(projected[:, :width], cosine, sine).astype(bf16)
        queries = queries * jnp.asarray(HEAD ** (-0.5), bf16)
        mixed, logs = attend(queries, kv, key_place, bounds)
        gate_up, down = mlp_weights(*after((by_y, down_parts), mixed))
        layers.append((gain_attn, gain_mlp, query_key, out_value, gate_up, down))
        middle = stream + matmul(mixed, out_value[:, :width])
        normed_mlp = (normalize(middle) * gain_mlp).astype(bf16)
        mine = matmul(normed_mlp, gate_up[0])
        other = matmul(normed_mlp, gate_up[1])
        gate, up = pick(mine, other), pick(other, mine)
        sigmoid = jax.nn.sigmoid(gate)
        hidden = (gate * sigmoid * up).astype(bf16)
        mine = matmul(hidden, down[0])
        other = matmul(hidden, down[1])
        saved.append((stream, normed, queries, kv, logs, mixed, middle, normed_mlp, gate, up, hidden))
        stream = middle + jnp.concatenate([pick(mine, other), pick(other, mine)], axis=1)
    output = stream.astype(bf16)

    latest = done = ()
    grad = cotangent.astype(f32)
    results = [None] * DECODER_LAYERS
    for l in reversed(range(DECODER_LAYERS)):
        gain_attn, gain_mlp, query_key, out_value, gate_up, down = layers[l]
        stream, normed, queries, kv, logs, mixed, middle, normed_mlp, gate, up, hidden = saved[l]
        grad_low = grad.astype(bf16)
        grad_a, grad_b = grad_low[:, :half_width], grad_low[:, half_width:]
        grad_mine, grad_other = pick(grad_a, grad_b), pick(grad_b, grad_a)
        down_received = swap_core(cross_rows(hidden, grad_other).astype(bf16))
        down_sum = (cross_rows(hidden, grad_mine) + down_received.astype(f32)).astype(bf16)

        dhidden = matmul_nt(grad_mine, down[0]) + matmul_nt(grad_other, down[1])
        sigmoid = jax.nn.sigmoid(gate)
        dgate = (dhidden * up * sigmoid * (1.0 + gate * (1.0 - sigmoid))).astype(bf16)
        dup = (dhidden * gate * sigmoid).astype(bf16)
        dmine, dother = pick(dgate, dup), pick(dup, dgate)
        gate_up_received = swap_core(cross_rows(normed_mlp, dother).astype(bf16))
        gate_up_sum = cross_rows(normed_mlp, dmine) + gate_up_received.astype(f32)
        gate_up_sum = gate_up_sum.astype(bf16)

        dnormed = matmul_nt(dmine, gate_up[0]) + matmul_nt(dother, gate_up[1])
        dmiddle, mlp_gain_grad = normalize_back(middle, gain_mlp, dnormed)
        dmiddle = dmiddle + grad
        dmiddle_low = dmiddle.astype(bf16)
        dmixed = matmul_nt(dmiddle_low, out_value[:, :width]).astype(bf16)
        dmixed = after(dmixed, (down_sum, gate_up_sum))
        dq, dkv = attend_back(queries, kv, key_place, bounds, mixed, logs, dmixed)
        down_sum = sum_over_x(after(down_sum, latest))
        dkv = after(scatter_pack(dkv), done)
        columns = gate_up_sum.shape[1] // 4
        gate_up_sum = sum_over_y(
            lambda k: lax.dynamic_slice_in_dim(gate_up_sum, k * columns, columns, axis=1)
        )
        gate_up_sum = sum_over_x(after(gate_up_sum, down_sum))
        dq = rotary_back(dq, cosine, sine).astype(bf16)
        dk = rotary_back(dkv[:, :key_width], cosine, sine).astype(bf16)
        dv = dkv[:, key_width:].astype(bf16)

        dqk = jnp.concatenate([dq, dk], axis=1)
        dnormed = matmul_nt(dqk, query_key) + matmul_nt(dv, out_value[:, width:])
        dstream, attn_gain_grad = normalize_back(stream, gain_attn, dnormed)
        grad = dstream + dmiddle

        def att_terms(first):
            wide = cross_rows(
                jnp.where(first, normed, mixed), jnp.where(first, dq, dmiddle_low)
            )
            return jnp.concatenate([wide, cross_rows(normed, jnp.where(first, dk, dv))], axis=1)

        received = swap_core(att_terms(jnp.logical_not(first_core)).astype(bf16))
        att_sum = (att_terms(first_core) + received.astype(f32)).astype(bf16)
        gain_grads = jnp.stack([attn_gain_grad, mlp_gain_grad]).astype(bf16)
        received = swap_core(gain_grads)
        gain_grads = (gain_grads.astype(f32) + received.astype(f32)).astype(bf16)
        gain_grads = gain_grads.reshape(2, -1, shard).swapaxes(0, 1)
        gain_grads = jnp.pad(gain_grads, ((0, 0), (0, 6), (0, att_width - shard)))
        att_sum = jnp.concatenate([att_sum.reshape(-1, shard, att_width), gain_grads], axis=1)
        att_sum = sum_over_x(after(att_sum.reshape(-1, att_width), gate_up_sum))
        latest = att_sum

        att_pair = att_sum.reshape(2, shard + 8, att_width)
        down_pair = down_sum.reshape(2, -1, half_width)
        gate_up_pair = gate_up_sum.reshape(2, shard, columns)
        if l > 0:
            done = finish_sums([att_pair, down_pair], gate_up_pair)
            (att_own, down_own, gate_up_own), (att_other, down_other, gate_up_other) = done
        else:
            mlp = finish_sums([down_pair], gate_up_pair)
            (down_own, gate_up_own), (down_other, gate_up_other) = mlp
            (att_own,), (att_other,) = finish_sums([att_pair], None)
        att_a, att_b = pick(att_own, att_other), pick(att_other, att_own)
        results[l] = (
            att_own[shard, :shard],
            att_a[:shard, :width],
            att_a[:shard, width:],
            att_b[:shard, width:],
            att_b[:shard, :width],
            att_own[shard + 1, :shard],
            pick(gate_up_own, gate_up_other),
            pick(gate_up_other, gate_up_own),
            jnp.concatenate([pick(down_own, down_other), pick(down_other, down_own)], axis=1),
        )
    stacked = [
        jnp.stack([results[l][m].astype(f32) for l in range(DECODER_LAYERS)], axis=0)
        for m in range(9)
    ]
    return (output, grad, *stacked)


def solution(mesh):
    weights = P(None, "fsdp", None)
    gains = P(None, "fsdp")
    packed = P(("rep", "fsdp"), None)
    in_specs = (
        packed,
        P("rep", None),
        gains,
        weights,
        weights,
        weights,
        weights,
        gains,
        weights,
        weights,
        weights,
        packed,
    )
    out_specs = (
        packed,
        packed,
        gains,
        weights,
        weights,
        weights,
        weights,
        gains,
        weights,
        weights,
        weights,
    )
    return jax.shard_map(body, mesh=mesh, in_specs=in_specs, out_specs=out_specs, check_vma=False)
```

```python
import functools

import jax
import jax.numpy as jnp
from jax import lax
from jax.experimental import pallas as pl
from jax.experimental.pallas import tpu as pltpu
from jax.sharding import PartitionSpec as P

QUERY_HEADS = 15
KEY_VALUE_HEADS = 5
GROUP = QUERY_HEADS // KEY_VALUE_HEADS
HEAD = 64
DECODER_LAYERS = 2
X_SIZE = 4

epsilon_norm = 1e-05
rope_base = 100000.0
masked_score = -1e30

f32 = jnp.float32
bf16 = jnp.bfloat16

NT = (((1,), (1,)), ((), ()))


def swap(array, axis, mask):
    count = lax.axis_size(axis)
    return lax.ppermute(array, axis, [(i, i ^ mask) for i in range(count)])


def swap_core(array):
    return swap(array, "rep", 1)


def gather_pack(rows):
    pair = jnp.stack([rows, swap(rows, "fsdp", 4)])
    parts = [pair] + [swap(pair, "fsdp", m) for m in range(1, X_SIZE)]
    return jnp.concatenate(parts, axis=0).reshape(-1, rows.shape[-1])


BLOCK_ORDER = (0, 4, 1, 5, 2, 6, 3, 7)


def scatter_pack(rows):
    blocks = rows.reshape(X_SIZE, 2, -1, rows.shape[-1])
    total = blocks[0].astype(f32)
    for m in range(1, X_SIZE):
        total = total + swap(blocks[m], "fsdp", m).astype(f32)
    return total[0] + swap(total[1].astype(bf16), "fsdp", 4).astype(f32)


def x_groups():
    return [[z * X_SIZE + x for x in range(X_SIZE)] for z in range(2)]


def sum_over_x(rows):
    return lax.psum_scatter(
        rows, "fsdp", scatter_dimension=0, tiled=True, axis_index_groups=x_groups()
    )


def to_owners(pair):
    z_hi = lax.axis_index("fsdp") // X_SIZE
    even = jnp.where(z_hi == 0, pair[0], pair[1])
    odd = jnp.where(z_hi == 0, pair[1], pair[0])
    reps, count = lax.axis_size("rep"), lax.axis_size("fsdp")

    def send(block, flip, z_lo):
        moves = []
        for rep in range(reps):
            for f in range(count):
                owner = 2 * (f % X_SIZE) + ((f // X_SIZE) ^ flip)
                moves.append((rep * count + f, (rep ^ (2 * z_lo)) * count + owner))
        return lax.ppermute(block, ("rep", "fsdp"), moves).astype(f32)

    near = send(even, 0, 0) + send(odd, 1, 0)
    far = send(even, 0, 1) + send(odd, 1, 1)
    return (near + far).astype(bf16)


def y_position():
    return lax.axis_index("rep") // 4


def sum_over_y(block_of):
    y = y_position()
    total = block_of(y).astype(f32)
    for m in range(1, 4):
        total = total + swap(block_of(jnp.bitwise_xor(y, m)), "rep", 4 * m).astype(f32)
    return total.astype(bf16)


def spread_over_y(block, axis):
    y = y_position()
    parts = [block] + [swap(block, "rep", 4 * m) for m in range(1, 4)]
    parts = [jnp.where(y % 2 == 1, parts[m ^ 1], parts[m]) for m in range(4)]
    parts = [jnp.where(y >= 2, parts[m ^ 2], parts[m]) for m in range(4)]
    return jnp.concatenate(parts, axis=axis)


LAST = 640


def as_rows(array):
    columns = array.shape[2]
    parts = []
    for first in range(0, columns, LAST):
        part = array[:, :, first : first + LAST]
        parts.append(jnp.pad(part, ((0, 0), (0, 0), (0, LAST - part.shape[2]))))
    return jnp.concatenate(parts, axis=1)


def rows_over_y(summed):
    joined = jnp.concatenate([as_rows(array) for array in summed], axis=1)
    blocks = joined.reshape(2, 4, joined.shape[1] // 4, LAST)
    return sum_over_y(lambda k: lax.dynamic_index_in_dim(blocks, k, axis=1, keepdims=False))


def whole_sums(over_y, shapes):
    own = spread_over_y(to_owners(over_y), 0)

    def take_apart(rows):
        results, first = [], 0
        for count, columns in shapes:
            parts = []
            for start in range(0, columns, LAST):
                parts.append(rows[first : first + count, : min(LAST, columns - start)])
                first += count
            results.append(jnp.concatenate(parts, axis=1))
        return results

    return take_apart(own), take_apart(swap_core(own))


def kernel_params():
    return pltpu.CompilerParams(vmem_limit_bytes=48 * 1024 * 1024)


def assemble_kernel(count, y_parts, ready_ref, *refs):
    parts, out, sems = refs[:count], refs[count], refs[count + 1]
    me = lax.axis_index("fsdp")
    copies = []
    if y_parts:
        y = lax.axis_index("rep") // 4
        columns = parts[0].shape[-1]
        for m in range(count):
            first = pl.multiple_of(jnp.bitwise_xor(y, m) * columns, 128)
            for k, block in enumerate(BLOCK_ORDER):
                place = out.at[jnp.bitwise_xor(me, block), :, pl.ds(first, columns)]
                copies.append((parts[m].at[k], place))
    else:
        for k, block in enumerate(BLOCK_ORDER):
            copies.append((parts[k // 2].at[k % 2], out.at[jnp.bitwise_xor(me, block)]))
    copies = [
        pltpu.make_async_copy(source, place, sems.at[i])
        for i, (source, place) in enumerate(copies)
    ]
    for copy in copies:
        copy.start()
    for copy in copies:
        copy.wait()


def assemble(parts, y_parts, *earlier):
    ready = token(earlier).reshape(1)
    rows, columns = parts[0].shape[1:]
    blocks = len(BLOCK_ORDER)
    columns = columns * len(parts) if y_parts else columns
    size = blocks * rows * columns * 4
    return pl.pallas_call(
        functools.partial(assemble_kernel, len(parts), y_parts),
        out_shape=jax.ShapeDtypeStruct((blocks, rows, columns), parts[0].dtype),
        in_specs=[pl.BlockSpec(memory_space=pltpu.SMEM)]
        + [pl.BlockSpec(memory_space=pl.ANY)] * len(parts),
        out_specs=pl.BlockSpec(memory_space=pltpu.VMEM),
        compiler_params=kernel_params(),
        scratch_shapes=[pltpu.SemaphoreType.DMA((blocks * (len(parts) if y_parts else 1),))],
        cost_estimate=pl.CostEstimate(flops=0, bytes_accessed=size, transcendentals=0),
        name="assemble",
    )(ready, *parts)


def token(arrays):
    total = jnp.zeros((), f32)
    for array in arrays:
        last = lax.slice(array, tuple(n - 1 for n in array.shape), array.shape).reshape(())
        total = total + (last != last).astype(f32)
    return total


def after(array, *earlier):
    return array + token(earlier).astype(array.dtype) if earlier else array


def z_pair(part):
    return jnp.stack([part, swap(part, "fsdp", 4)])


def gather_blocks(pair, *earlier):
    pair = after(pair, *earlier)
    return [pair] + [swap(pair, "fsdp", m) for m in range(1, X_SIZE)]


def quarter_by_y(part):
    columns = part.shape[1] // 4
    return lax.dynamic_slice_in_dim(part, y_position() * columns, columns, axis=1)


def gather_by_y(blocks, earlier, later):
    joined = after(jnp.concatenate(blocks, axis=0), earlier)
    near = [swap(joined, "rep", 4 * m) for m in (1, 2)]
    return [joined, *near, swap(after(joined, later), "rep", 12)]


def stacked_heads(array, kv_head):
    first = kv_head * GROUP
    return jnp.concatenate(
        [array[:, (first + g) * HEAD : (first + g + 1) * HEAD] for g in range(GROUP)], axis=0
    )


def attention_forward_kernel(q_ref, kv_ref, key_place_ref, bounds_ref, mixed_ref, log_ref, bias):
    rows = q_ref.shape[0]
    keys = kv_ref.shape[0]
    width = KEY_VALUE_HEADS * HEAD
    place = key_place_ref[...]
    bias[...] = jnp.where(
        (place >= bounds_ref[0:1, :]) & (place <= bounds_ref[1:2, :]), 0.0, masked_score
    )
    for h in range(KEY_VALUE_HEADS):
        queries = stacked_heads(q_ref[...], h)
        keys_h = kv_ref[:, h * HEAD : (h + 1) * HEAD]
        values_h = kv_ref[:, width + h * HEAD : width + (h + 1) * HEAD]
        scores = lax.dot_general(keys_h, queries, NT, preferred_element_type=f32) + bias[...]
        top = jnp.max(scores, axis=0, keepdims=True)
        weights = jnp.exp(scores - top)
        total = jnp.sum(weights, axis=0, keepdims=True)
        mixed = jnp.dot(
            values_h.T, weights.astype(bf16), preferred_element_type=f32
        ) * (1.0 / total)
        mixed = mixed.T.astype(bf16)
        for g in range(GROUP):
            j = h * GROUP + g
            mixed_ref[:, j * HEAD : (j + 1) * HEAD] = mixed[g * rows : (g + 1) * rows]
        log_ref[h : h + 1, :] = top + jnp.log(total)


def attention_backward_kernel(
    q_ref, kv_ref, key_place_ref, bounds_ref, mixed_ref, log_ref, grad_ref, dq_ref, dkv_ref
):
    rows = q_ref.shape[0]
    keys = kv_ref.shape[0]
    width = KEY_VALUE_HEADS * HEAD
    chunk = keys // 4
    for h in range(KEY_VALUE_HEADS):
        queries = stacked_heads(q_ref[...], h)
        grads = stacked_heads(grad_ref[...], h)
        mixed = stacked_heads(mixed_ref[...], h)
        product = (grads.astype(f32) * mixed.astype(f32)).T
        delta = jnp.sum(product, axis=0, keepdims=True)
        logs = log_ref[h : h + 1, :]
        dq = jnp.zeros((HEAD, GROUP * rows), f32)
        for part in range(4):
            span = slice(part * chunk, (part + 1) * chunk)
            place = key_place_ref[span, :]
            allowed = (place >= bounds_ref[0:1, :]) & (place <= bounds_ref[1:2, :])
            keys_h = kv_ref[span, h * HEAD : (h + 1) * HEAD]
            values_h = kv_ref[span, width + h * HEAD : width + (h + 1) * HEAD]
            scores = lax.dot_general(keys_h, queries, NT, preferred_element_type=f32)
            weights = jnp.exp(jnp.where(allowed, scores, masked_score) - logs)
            dweights = lax.dot_general(values_h, grads, NT, preferred_element_type=f32)
            dscores = (weights * (dweights - delta)).astype(bf16)
            dvalues = jnp.dot(weights.astype(bf16), grads, preferred_element_type=f32)
            dkeys = jnp.dot(dscores, queries, preferred_element_type=f32)
            dq = dq + jnp.dot(keys_h.T, dscores, preferred_element_type=f32)
            dkv_ref[span, h * HEAD : (h + 1) * HEAD] = dkeys.astype(bf16)
            dkv_ref[span, width + h * HEAD : width + (h + 1) * HEAD] = dvalues.astype(bf16)
        dq = dq.T * HEAD ** (-0.5)
        for g in range(GROUP):
            j = h * GROUP + g
            dq_ref[:, j * HEAD : (j + 1) * HEAD] = dq[g * rows : (g + 1) * rows]


def attend(queries, kv, key_place, bounds):
    rows, keys = queries.shape[0], kv.shape[0]
    pairs = QUERY_HEADS * rows * keys
    return pl.pallas_call(
        attention_forward_kernel,
        out_shape=(
            jax.ShapeDtypeStruct(queries.shape, bf16),
            jax.ShapeDtypeStruct((8, GROUP * rows), f32),
        ),
        scratch_shapes=[pltpu.VMEM((keys, GROUP * rows), f32)],
        compiler_params=kernel_params(),
        cost_estimate=pl.CostEstimate(
            flops=4 * pairs * HEAD, bytes_accessed=4 * 1024 * 1024, transcendentals=pairs
        ),
        name="attention_forward",
    )(queries, kv, key_place, bounds)


def attend_back(queries, kv, key_place, bounds, mixed, logs, grads):
    rows, keys = queries.shape[0], kv.shape[0]
    pairs = QUERY_HEADS * rows * keys
    return pl.pallas_call(
        attention_backward_kernel,
        out_shape=(
            jax.ShapeDtypeStruct(queries.shape, f32),
            jax.ShapeDtypeStruct(kv.shape, bf16),
        ),
        compiler_params=kernel_params(),
        cost_estimate=pl.CostEstimate(
            flops=10 * pairs * HEAD, bytes_accessed=6 * 1024 * 1024, transcendentals=pairs
        ),
        name="attention_backward",
    )(queries, kv, key_place, bounds, mixed, logs, grads)


def normalize(stream):
    return stream * lax.rsqrt(jnp.mean(stream * stream, axis=-1, keepdims=True) + epsilon_norm)


def normalize_back(stream, gain, grad):
    inverse = lax.rsqrt(jnp.mean(stream * stream, axis=-1, keepdims=True) + epsilon_norm)
    unit = stream * inverse
    scaled = grad * gain
    gain_grad = jnp.sum(grad * unit, axis=0)
    return inverse * (scaled - unit * jnp.mean(scaled * unit, axis=-1, keepdims=True)), gain_grad


def turn(flat):
    half = HEAD // 2
    ahead = jnp.concatenate([flat[:, half:], flat[:, :half]], axis=1)
    behind = jnp.concatenate([flat[:, -half:], flat[:, :-half]], axis=1)
    lane = lax.broadcasted_iota(jnp.int32, flat.shape, 1) % HEAD
    return jnp.where(lane < half, -ahead, behind)


def rotary(flat, cosine, sine):
    return flat * cosine[:, : flat.shape[1]] + turn(flat) * sine[:, : flat.shape[1]]


def rotary_back(flat, cosine, sine):
    return flat * cosine[:, : flat.shape[1]] - turn(flat * sine[:, : flat.shape[1]])


def matmul(left, right):
    return jnp.dot(left, right, preferred_element_type=f32)


def matmul_nt(left, right):
    return lax.dot_general(left, right, NT, preferred_element_type=f32)


def cross_rows(left, right):
    return lax.dot_general(left, right, (((0,), (0,)), ((), ())), preferred_element_type=f32)


def body(
    tokens,
    seq_lengths,
    attn_gain,
    query_weight,
    key_projection,
    value_projection,
    out_weight,
    mlp_gain,
    gate_weight,
    up_weight,
    down_weight,
    cotangent,
):
    rows, width = tokens.shape
    shard = query_weight.shape[1]
    key_width = key_projection.shape[2]
    att_width = width + key_width
    half_width = width // 2
    me = lax.axis_index("fsdp")
    first_core = lax.axis_index("rep") % 2 == 0

    def pick(a, b):
        return jnp.where(first_core, a, b)

    lengths = seq_lengths[0]
    ends = jnp.cumsum(lengths)
    starts = ends - lengths
    places = me * rows + jnp.arange(rows, dtype=jnp.int32)
    segment = jnp.sum((places[:, None] >= ends[None, :-1]).astype(jnp.int32), axis=1)
    chosen = segment[:, None] == jnp.arange(lengths.shape[0], dtype=jnp.int32)[None, :]
    start = jnp.sum(chosen.astype(jnp.int32) * starts[None, :], axis=1)
    offsets = (places - start).astype(f32)
    frequency = rope_base ** (-(jnp.arange(HEAD // 2, dtype=f32) * 2.0) / HEAD)
    angles = offsets[:, None] * frequency[None, :]
    cosine = jnp.tile(jnp.cos(angles), (1, 2 * QUERY_HEADS))
    sine = jnp.tile(jnp.sin(angles), (1, 2 * QUERY_HEADS))
    bounds = jnp.stack([jnp.tile(start, GROUP), jnp.tile(places, GROUP)])
    bounds = jnp.pad(bounds, ((0, 6), (0, 0)))
    blocks = jnp.bitwise_xor(me, jnp.array(BLOCK_ORDER, jnp.int32))
    key_place = blocks[:, None] * rows + jnp.arange(rows, dtype=jnp.int32)[None, :]
    key_place = key_place.reshape(-1, 1)

    def own_weights(l, *earlier):
        gains = jnp.stack([attn_gain[l], mlp_gain[l]])
        gains = jnp.pad(gains, ((0, 6), (0, att_width - shard)))
        att = pick(
            jnp.concatenate([query_weight[l], key_projection[l]], axis=1),
            jnp.concatenate([out_weight[l], value_projection[l]], axis=1),
        )
        att = jnp.concatenate([att, gains], axis=0)
        gate_up = pick(gate_weight[l], up_weight[l])
        down = pick(down_weight[l][:, :half_width], down_weight[l][:, half_width:])
        return after(att, *earlier), after(gate_up, *earlier), after(down, *earlier)

    def gather_parts(own, *earlier):
        att, gate_up, down = own
        att_parts = gather_blocks(z_pair(att), *earlier)
        return att_parts, gather_blocks(z_pair(quarter_by_y(gate_up)), *earlier), z_pair(down)

    def attention_weights(att_parts, *earlier):
        mine = assemble(att_parts, False, *earlier)
        other = swap_core(mine)
        gain_attn = mine[:, shard, :shard].reshape(width).astype(f32)
        gain_mlp = mine[:, shard + 1, :shard].reshape(width).astype(f32)
        mine = mine[:, :shard].reshape(width, att_width)
        other = other[:, :shard].reshape(width, att_width)
        return gain_attn, gain_mlp, pick(mine, other), pick(other, mine)

    def mlp_weights(by_y, down_parts, mixed):
        mine = assemble(by_y, True, mixed).reshape(width, -1)
        gate_up = (mine, swap_core(mine))
        mine = assemble(down_parts, False, mixed).reshape(-1, half_width)
        return gate_up, (mine, swap_core(mine))

    stream = tokens.astype(f32)
    saved = []
    layers = []
    parts = gather_parts(own_weights(0))
    for l in range(DECODER_LAYERS):
        att_parts, quarters, down_pair = parts
        gain_attn, gain_mlp, query_key, out_value = attention_weights(
            att_parts, stream, *quarters
        )
        normed = (normalize(stream) * gain_attn).astype(bf16)
        values = matmul(normed, out_value[:, width:]).astype(bf16)
        projected = matmul(normed, query_key)
        keys = rotary(projected[:, width:], cosine, sine).astype(bf16)
        kv = gather_pack(after(jnp.concatenate([keys, values], axis=1), down_pair))
        by_y = gather_by_y(quarters, projected, kv)
        down_parts = gather_blocks(down_pair, kv)
        queries = rotary(projected[:, :width], cosine, sine).astype(bf16)
        queries = queries * jnp.asarray(HEAD ** (-0.5), bf16)
        if l + 1 < DECODER_LAYERS:
            parts = gather_parts(own_weights(l + 1, projected), kv)
        mixed, logs = attend(queries, kv, key_place, bounds)
        gate_up, down = mlp_weights(by_y, down_parts, mixed)
        layers.append((gain_attn, gain_mlp, query_key, out_value, gate_up, down))
        middle = stream + matmul(mixed, out_value[:, :width])
        normed_mlp = (normalize(middle) * gain_mlp).astype(bf16)
        mine = matmul(normed_mlp, gate_up[0])
        other = matmul(normed_mlp, gate_up[1])
        gate, up = pick(mine, other), pick(other, mine)
        sigmoid = jax.nn.sigmoid(gate)
        hidden = (gate * sigmoid * up).astype(bf16)
        mine = matmul(hidden, down[0])
        other = matmul(hidden, down[1])
        saved.append((stream, normed, queries, kv, logs, mixed, middle, normed_mlp, gate, up, hidden))
        stream = middle + jnp.concatenate([pick(mine, other), pick(other, mine)], axis=1)
    output = stream.astype(bf16)

    done = ()
    pending = []
    grad = cotangent.astype(f32)
    results = [None] * DECODER_LAYERS
    for l in reversed(range(DECODER_LAYERS)):
        gain_attn, gain_mlp, query_key, out_value, gate_up, down = layers[l]
        stream, normed, queries, kv, logs, mixed, middle, normed_mlp, gate, up, hidden = saved[l]
        grad_low = grad.astype(bf16)
        grad_a, grad_b = grad_low[:, :half_width], grad_low[:, half_width:]
        grad_mine, grad_other = pick(grad_a, grad_b), pick(grad_b, grad_a)
        down_received = swap_core(cross_rows(hidden, grad_other).astype(bf16))
        down_sum = (cross_rows(hidden, grad_mine) + down_received.astype(f32)).astype(bf16)

        dhidden = matmul_nt(grad_mine, down[0]) + matmul_nt(grad_other, down[1])
        sigmoid = jax.nn.sigmoid(gate)
        dgate = (dhidden * up * sigmoid * (1.0 + gate * (1.0 - sigmoid))).astype(bf16)
        dup = (dhidden * gate * sigmoid).astype(bf16)
        dmine, dother = pick(dgate, dup), pick(dup, dgate)
        gate_up_received = swap_core(cross_rows(normed_mlp, dother).astype(bf16))
        gate_up_sum = cross_rows(normed_mlp, dmine) + gate_up_received.astype(f32)
        gate_up_sum = gate_up_sum.astype(bf16)

        dnormed = matmul_nt(dmine, gate_up[0]) + matmul_nt(dother, gate_up[1])
        dmiddle, mlp_gain_grad = normalize_back(middle, gain_mlp, dnormed)
        dmiddle = dmiddle + grad
        dmiddle_low = dmiddle.astype(bf16)
        dmixed = matmul_nt(dmiddle_low, out_value[:, :width]).astype(bf16)
        dmixed = after(dmixed, down_sum, gate_up_sum)
        dq, dkv = attend_back(queries, kv, key_place, bounds, mixed, logs, dmixed)
        down_sum = sum_over_x(down_sum)
        gate_up_sum = sum_over_x(gate_up_sum)
        dkv = scatter_pack(dkv)
        dq = rotary_back(dq, cosine, sine).astype(bf16)
        dk = rotary_back(dkv[:, :key_width], cosine, sine).astype(bf16)
        dv = dkv[:, key_width:].astype(bf16)

        dqk = after(jnp.concatenate([dq, dk], axis=1), *done)
        dnormed = matmul_nt(dqk, query_key) + matmul_nt(dv, out_value[:, width:])
        dstream, attn_gain_grad = normalize_back(stream, gain_attn, dnormed)
        grad = dstream + dmiddle

        def att_terms(first):
            wide = cross_rows(
                jnp.where(first, normed, mixed), jnp.where(first, dq, dmiddle_low)
            )
            return jnp.concatenate([wide, cross_rows(normed, jnp.where(first, dk, dv))], axis=1)

        received = swap_core(att_terms(jnp.logical_not(first_core)).astype(bf16))
        att_sum = (att_terms(first_core) + received.astype(f32)).astype(bf16)
        gain_grads = jnp.stack([attn_gain_grad, mlp_gain_grad]).astype(bf16)
        received = swap_core(gain_grads)
        gain_grads = (gain_grads.astype(f32) + received.astype(f32)).astype(bf16)
        gain_grads = gain_grads.reshape(2, -1, shard).swapaxes(0, 1)
        gain_grads = jnp.pad(gain_grads, ((0, 0), (0, 6), (0, att_width - shard)))
        att_sum = jnp.concatenate([att_sum.reshape(-1, shard, att_width), gain_grads], axis=1)
        att_sum = after(att_sum.reshape(-1, att_width), gate_up_sum)
        late = att_sum
        att_sum = sum_over_x(att_sum)

        att_pair = att_sum.reshape(2, shard + 8, att_width)
        down_pair = down_sum.reshape(2, -1, half_width)
        gate_up_pair = gate_up_sum.reshape(2, shard, -1)
        if l > 0:
            groups = [(l, (att_pair, down_pair, gate_up_pair))]
        else:
            groups = [(l, (down_pair, gate_up_pair)), (l, (att_pair,))]
        for layer, arrays in groups:
            shapes = [array.shape[1:] for array in arrays]
            pending.append((layer, rows_over_y(arrays), shapes))
        done = (pending[-1][1],)

    found = {}
    for layer, over_y, shapes in pending:
        if shapes != pending[-1][2]:
            over_y = after(over_y, late)
        own, other = whole_sums(over_y, shapes)
        for shape, pair in zip(shapes, zip(own, other)):
            found[layer, shape] = pair
    att_shape = (shard + 8, att_width)
    down_shape = (down_weight.shape[1], half_width)
    gate_up_shape = (shard, gate_weight.shape[2])
    for l in range(DECODER_LAYERS):
        att_own, att_other = found[l, att_shape]
        down_own, down_other = found[l, down_shape]
        gate_up_own, gate_up_other = found[l, gate_up_shape]
        att_a, att_b = pick(att_own, att_other), pick(att_other, att_own)
        results[l] = (
            att_own[shard, :shard],
            att_a[:shard, :width],
            att_a[:shard, width:],
            att_b[:shard, width:],
            att_b[:shard, :width],
            att_own[shard + 1, :shard],
            pick(gate_up_own, gate_up_other),
            pick(gate_up_other, gate_up_own),
            jnp.concatenate([pick(down_own, down_other), pick(down_other, down_own)], axis=1),
        )
    stacked = [
        jnp.stack([results[l][m].astype(f32) for l in range(DECODER_LAYERS)], axis=0)
        for m in range(9)
    ]
    return (output, grad, *stacked)


def solution(mesh):
    weights = P(None, "fsdp", None)
    gains = P(None, "fsdp")
    packed = P(("rep", "fsdp"), None)
    in_specs = (
        packed,
        P("rep", None),
        gains,
        weights,
        weights,
        weights,
        weights,
        gains,
        weights,
        weights,
        weights,
        packed,
    )
    out_specs = (
        packed,
        packed,
        gains,
        weights,
        weights,
        weights,
        weights,
        gains,
        weights,
        weights,
        weights,
    )
    return jax.shard_map(body, mesh=mesh, in_specs=in_specs, out_specs=out_specs, check_vma=False)
```

```python
import functools

import jax
import jax.numpy as jnp
from jax import lax
from jax.experimental import pallas as pl
from jax.experimental.pallas import tpu as pltpu
from jax.sharding import PartitionSpec as P

QUERY_HEADS = 15
KEY_VALUE_HEADS = 5
GROUP = QUERY_HEADS // KEY_VALUE_HEADS
HEAD = 64
DECODER_LAYERS = 2
X_SIZE = 4

epsilon_norm = 1e-05
rope_base = 100000.0
masked_score = -1e30

f32 = jnp.float32
bf16 = jnp.bfloat16

NT = (((1,), (1,)), ((), ()))


def swap(array, axis, mask):
    count = lax.axis_size(axis)
    return lax.ppermute(array, axis, [(i, i ^ mask) for i in range(count)])


def swap_core(array):
    return swap(array, "rep", 1)


def gather_pack(rows):
    pair = jnp.stack([rows, swap(rows, "fsdp", 4)])
    parts = [pair] + [swap(pair, "fsdp", m) for m in range(1, X_SIZE)]
    return jnp.concatenate(parts, axis=0).reshape(-1, rows.shape[-1])


BLOCK_ORDER = (0, 4, 1, 5, 2, 6, 3, 7)


def scatter_pack(rows):
    blocks = rows.reshape(X_SIZE, 2, -1, rows.shape[-1])
    total = blocks[0].astype(f32)
    for m in range(1, X_SIZE):
        total = total + swap(blocks[m], "fsdp", m).astype(f32)
    return total[0] + swap(total[1].astype(bf16), "fsdp", 4).astype(f32)


def x_groups():
    return [[z * X_SIZE + x for x in range(X_SIZE)] for z in range(2)]


def sum_over_x(rows):
    return lax.psum_scatter(
        rows, "fsdp", scatter_dimension=0, tiled=True, axis_index_groups=x_groups()
    )


def to_owners(pair):
    z_hi = lax.axis_index("fsdp") // X_SIZE
    even = jnp.where(z_hi == 0, pair[0], pair[1])
    odd = jnp.where(z_hi == 0, pair[1], pair[0])
    reps, count = lax.axis_size("rep"), lax.axis_size("fsdp")

    def send(block, flip, z_lo):
        moves = []
        for rep in range(reps):
            for f in range(count):
                owner = 2 * (f % X_SIZE) + ((f // X_SIZE) ^ flip)
                moves.append((rep * count + f, (rep ^ (2 * z_lo)) * count + owner))
        return lax.ppermute(block, ("rep", "fsdp"), moves).astype(f32)

    near = send(even, 0, 0) + send(odd, 1, 0)
    far = send(even, 0, 1) + send(odd, 1, 1)
    return (near + far).astype(bf16)


def y_position():
    return lax.axis_index("rep") // 4


def sum_over_y(block_of):
    y = y_position()
    total = block_of(y).astype(f32)
    for m in range(1, 4):
        total = total + swap(block_of(jnp.bitwise_xor(y, m)), "rep", 4 * m).astype(f32)
    return total.astype(bf16)


def spread_over_y(block, axis):
    y = y_position()
    parts = [block] + [swap(block, "rep", 4 * m) for m in range(1, 4)]
    parts = [jnp.where(y % 2 == 1, parts[m ^ 1], parts[m]) for m in range(4)]
    parts = [jnp.where(y >= 2, parts[m ^ 2], parts[m]) for m in range(4)]
    return jnp.concatenate(parts, axis=axis)


LAST = 640


def as_rows(array):
    columns = array.shape[2]
    parts = []
    for first in range(0, columns, LAST):
        part = array[:, :, first : first + LAST]
        parts.append(jnp.pad(part, ((0, 0), (0, 0), (0, LAST - part.shape[2]))))
    return jnp.concatenate(parts, axis=1)


def finish_sums(summed):
    joined = jnp.concatenate([as_rows(array) for array in summed], axis=1)
    blocks = joined.reshape(2, 4, joined.shape[1] // 4, LAST)
    total = sum_over_y(lambda k: lax.dynamic_index_in_dim(blocks, k, axis=1, keepdims=False))
    own = spread_over_y(to_owners(total), 0)

    def take_apart(rows):
        results, first = [], 0
        for array in summed:
            count, columns = array.shape[1:]
            parts = []
            for start in range(0, columns, LAST):
                parts.append(rows[first : first + count, : min(LAST, columns - start)])
                first += count
            results.append(jnp.concatenate(parts, axis=1))
        return results

    return take_apart(own), take_apart(swap_core(own))


def kernel_params():
    return pltpu.CompilerParams(vmem_limit_bytes=48 * 1024 * 1024)


def assemble_kernel(count, y_parts, *refs):
    parts, out, sems = refs[:count], refs[count], refs[count + 1]
    me = lax.axis_index("fsdp")
    copies = []
    if y_parts:
        y = lax.axis_index("rep") // 4
        columns = parts[0].shape[-1]
        for m in range(count):
            first = pl.multiple_of(jnp.bitwise_xor(y, m) * columns, 128)
            for k, block in enumerate(BLOCK_ORDER):
                place = out.at[jnp.bitwise_xor(me, block), :, pl.ds(first, columns)]
                copies.append((parts[m].at[k], place))
    else:
        for k, block in enumerate(BLOCK_ORDER):
            copies.append((parts[k // 2].at[k % 2], out.at[jnp.bitwise_xor(me, block)]))
    copies = [
        pltpu.make_async_copy(source, place, sems.at[i])
        for i, (source, place) in enumerate(copies)
    ]
    for copy in copies:
        copy.start()
    for copy in copies:
        copy.wait()


def assemble(parts, y_parts):
    rows, columns = parts[0].shape[1:]
    blocks = len(BLOCK_ORDER)
    columns = columns * len(parts) if y_parts else columns
    size = blocks * rows * columns * 4
    return pl.pallas_call(
        functools.partial(assemble_kernel, len(parts), y_parts),
        out_shape=jax.ShapeDtypeStruct((blocks, rows, columns), parts[0].dtype),
        in_specs=[pl.BlockSpec(memory_space=pl.ANY)] * len(parts),
        out_specs=pl.BlockSpec(memory_space=pltpu.VMEM),
        compiler_params=kernel_params(),
        scratch_shapes=[pltpu.SemaphoreType.DMA((blocks * (len(parts) if y_parts else 1),))],
        cost_estimate=pl.CostEstimate(flops=0, bytes_accessed=size, transcendentals=0),
        name="assemble",
    )(*parts)


def after(array, earlier):
    return lax.optimization_barrier((array, earlier))[0]


def gather_blocks(part, earlier):
    pair = jnp.stack([part, swap(part, "fsdp", 4)])
    pair = pair if earlier is None else after(pair, earlier)
    return [pair] + [swap(pair, "fsdp", m) for m in range(1, X_SIZE)]


def gather_by_y(part, earlier):
    columns = part.shape[1] // 4
    y = y_position()
    quarter = lax.dynamic_slice_in_dim(part, y * columns, columns, axis=1)
    blocks = gather_blocks(quarter, earlier)
    joined = jnp.concatenate(blocks, axis=0)
    parts = [joined] + [swap(joined, "rep", 4 * m) for m in range(1, 4)]
    return parts, joined


def stacked_heads(array, kv_head):
    first = kv_head * GROUP
    return jnp.concatenate(
        [array[:, (first + g) * HEAD : (first + g + 1) * HEAD] for g in range(GROUP)], axis=0
    )


def attention_forward_kernel(q_ref, kv_ref, key_place_ref, bounds_ref, mixed_ref, log_ref, bias):
    rows = q_ref.shape[0]
    keys = kv_ref.shape[0]
    width = KEY_VALUE_HEADS * HEAD
    place = key_place_ref[...]
    bias[...] = jnp.where(
        (place >= bounds_ref[0:1, :]) & (place <= bounds_ref[1:2, :]), 0.0, masked_score
    )
    for h in range(KEY_VALUE_HEADS):
        queries = stacked_heads(q_ref[...], h)
        keys_h = kv_ref[:, h * HEAD : (h + 1) * HEAD]
        values_h = kv_ref[:, width + h * HEAD : width + (h + 1) * HEAD]
        scores = lax.dot_general(keys_h, queries, NT, preferred_element_type=f32) + bias[...]
        top = jnp.max(scores, axis=0, keepdims=True)
        weights = jnp.exp(scores - top)
        total = jnp.sum(weights, axis=0, keepdims=True)
        mixed = jnp.dot(
            values_h.T, weights.astype(bf16), preferred_element_type=f32
        ) * (1.0 / total)
        mixed = mixed.T.astype(bf16)
        for g in range(GROUP):
            j = h * GROUP + g
            mixed_ref[:, j * HEAD : (j + 1) * HEAD] = mixed[g * rows : (g + 1) * rows]
        log_ref[h : h + 1, :] = top + jnp.log(total)


def attention_backward_kernel(
    q_ref, kv_ref, key_place_ref, bounds_ref, mixed_ref, log_ref, grad_ref, dq_ref, dkv_ref
):
    rows = q_ref.shape[0]
    keys = kv_ref.shape[0]
    width = KEY_VALUE_HEADS * HEAD
    chunk = keys // 4
    for h in range(KEY_VALUE_HEADS):
        queries = stacked_heads(q_ref[...], h)
        grads = stacked_heads(grad_ref[...], h)
        mixed = stacked_heads(mixed_ref[...], h)
        product = (grads.astype(f32) * mixed.astype(f32)).T
        delta = jnp.sum(product, axis=0, keepdims=True)
        logs = log_ref[h : h + 1, :]
        dq = jnp.zeros((HEAD, GROUP * rows), f32)
        for part in range(4):
            span = slice(part * chunk, (part + 1) * chunk)
            place = key_place_ref[span, :]
            allowed = (place >= bounds_ref[0:1, :]) & (place <= bounds_ref[1:2, :])
            keys_h = kv_ref[span, h * HEAD : (h + 1) * HEAD]
            values_h = kv_ref[span, width + h * HEAD : width + (h + 1) * HEAD]
            scores = lax.dot_general(keys_h, queries, NT, preferred_element_type=f32)
            weights = jnp.exp(jnp.where(allowed, scores, masked_score) - logs)
            dweights = lax.dot_general(values_h, grads, NT, preferred_element_type=f32)
            dscores = (weights * (dweights - delta)).astype(bf16)
            dvalues = jnp.dot(weights.astype(bf16), grads, preferred_element_type=f32)
            dkeys = jnp.dot(dscores, queries, preferred_element_type=f32)
            dq = dq + jnp.dot(keys_h.T, dscores, preferred_element_type=f32)
            dkv_ref[span, h * HEAD : (h + 1) * HEAD] = dkeys.astype(bf16)
            dkv_ref[span, width + h * HEAD : width + (h + 1) * HEAD] = dvalues.astype(bf16)
        dq = dq.T * HEAD ** (-0.5)
        for g in range(GROUP):
            j = h * GROUP + g
            dq_ref[:, j * HEAD : (j + 1) * HEAD] = dq[g * rows : (g + 1) * rows]


def attend(queries, kv, key_place, bounds):
    rows, keys = queries.shape[0], kv.shape[0]
    pairs = QUERY_HEADS * rows * keys
    return pl.pallas_call(
        attention_forward_kernel,
        out_shape=(
            jax.ShapeDtypeStruct(queries.shape, bf16),
            jax.ShapeDtypeStruct((8, GROUP * rows), f32),
        ),
        scratch_shapes=[pltpu.VMEM((keys, GROUP * rows), f32)],
        compiler_params=kernel_params(),
        cost_estimate=pl.CostEstimate(
            flops=4 * pairs * HEAD, bytes_accessed=4 * 1024 * 1024, transcendentals=pairs
        ),
        name="attention_forward",
    )(queries, kv, key_place, bounds)


def attend_back(queries, kv, key_place, bounds, mixed, logs, grads):
    rows, keys = queries.shape[0], kv.shape[0]
    pairs = QUERY_HEADS * rows * keys
    return pl.pallas_call(
        attention_backward_kernel,
        out_shape=(
            jax.ShapeDtypeStruct(queries.shape, f32),
            jax.ShapeDtypeStruct(kv.shape, bf16),
        ),
        compiler_params=kernel_params(),
        cost_estimate=pl.CostEstimate(
            flops=10 * pairs * HEAD, bytes_accessed=6 * 1024 * 1024, transcendentals=pairs
        ),
        name="attention_backward",
    )(queries, kv, key_place, bounds, mixed, logs, grads)


def normalize(stream):
    return stream * lax.rsqrt(jnp.mean(stream * stream, axis=-1, keepdims=True) + epsilon_norm)


def normalize_back(stream, gain, grad):
    inverse = lax.rsqrt(jnp.mean(stream * stream, axis=-1, keepdims=True) + epsilon_norm)
    unit = stream * inverse
    scaled = grad * gain
    gain_grad = jnp.sum(grad * unit, axis=0)
    return inverse * (scaled - unit * jnp.mean(scaled * unit, axis=-1, keepdims=True)), gain_grad


def turn(flat):
    half = HEAD // 2
    ahead = jnp.concatenate([flat[:, half:], flat[:, :half]], axis=1)
    behind = jnp.concatenate([flat[:, -half:], flat[:, :-half]], axis=1)
    lane = lax.broadcasted_iota(jnp.int32, flat.shape, 1) % HEAD
    return jnp.where(lane < half, -ahead, behind)


def rotary(flat, cosine, sine):
    return flat * cosine[:, : flat.shape[1]] + turn(flat) * sine[:, : flat.shape[1]]


def rotary_back(flat, cosine, sine):
    return flat * cosine[:, : flat.shape[1]] - turn(flat * sine[:, : flat.shape[1]])


def matmul(left, right):
    return jnp.dot(left, right, preferred_element_type=f32)


def matmul_nt(left, right):
    return lax.dot_general(left, right, NT, preferred_element_type=f32)


def cross_rows(left, right):
    return lax.dot_general(left, right, (((0,), (0,)), ((), ())), preferred_element_type=f32)


def body(
    tokens,
    seq_lengths,
    attn_gain,
    query_weight,
    key_projection,
    value_projection,
    out_weight,
    mlp_gain,
    gate_weight,
    up_weight,
    down_weight,
    cotangent,
):
    rows, width = tokens.shape
    shard = query_weight.shape[1]
    key_width = key_projection.shape[2]
    att_width = width + key_width
    half_width = width // 2
    me = lax.axis_index("fsdp")
    first_core = lax.axis_index("rep") % 2 == 0

    def pick(a, b):
        return jnp.where(first_core, a, b)

    lengths = seq_lengths[0]
    ends = jnp.cumsum(lengths)
    starts = ends - lengths
    places = me * rows + jnp.arange(rows, dtype=jnp.int32)
    segment = jnp.sum((places[:, None] >= ends[None, :-1]).astype(jnp.int32), axis=1)
    chosen = segment[:, None] == jnp.arange(lengths.shape[0], dtype=jnp.int32)[None, :]
    start = jnp.sum(chosen.astype(jnp.int32) * starts[None, :], axis=1)
    offsets = (places - start).astype(f32)
    frequency = rope_base ** (-(jnp.arange(HEAD // 2, dtype=f32) * 2.0) / HEAD)
    angles = offsets[:, None] * frequency[None, :]
    cosine = jnp.tile(jnp.cos(angles), (1, 2 * QUERY_HEADS))
    sine = jnp.tile(jnp.sin(angles), (1, 2 * QUERY_HEADS))
    bounds = jnp.stack([jnp.tile(start, GROUP), jnp.tile(places, GROUP)])
    bounds = jnp.pad(bounds, ((0, 6), (0, 0)))
    blocks = jnp.bitwise_xor(me, jnp.array(BLOCK_ORDER, jnp.int32))
    key_place = blocks[:, None] * rows + jnp.arange(rows, dtype=jnp.int32)[None, :]
    key_place = key_place.reshape(-1, 1)

    def own_weights(l):
        gains = jnp.stack([attn_gain[l], mlp_gain[l]])
        gains = jnp.pad(gains, ((0, 6), (0, att_width - shard)))
        att = pick(
            jnp.concatenate([query_weight[l], key_projection[l]], axis=1),
            jnp.concatenate([out_weight[l], value_projection[l]], axis=1),
        )
        att = jnp.concatenate([att, gains], axis=0)
        gate_up = pick(gate_weight[l], up_weight[l])
        down = pick(down_weight[l][:, :half_width], down_weight[l][:, half_width:])
        return att, gate_up, down

    def gather_parts(own):
        att, gate_up, down = own
        att_parts = gather_blocks(att, None)
        by_y, by_x = gather_by_y(gate_up, None)
        return att_parts, by_y, by_x, down

    def attention_weights(att_parts):
        mine = assemble(att_parts, False)
        other = swap_core(mine)
        gain_attn = mine[:, shard, :shard].reshape(width).astype(f32)
        gain_mlp = mine[:, shard + 1, :shard].reshape(width).astype(f32)
        mine = mine[:, :shard].reshape(width, att_width)
        other = other[:, :shard].reshape(width, att_width)
        return gain_attn, gain_mlp, pick(mine, other), pick(other, mine)

    def mlp_weights(by_y, down_parts):
        mine = assemble(by_y, True).reshape(width, -1)
        gate_up = (mine, swap_core(mine))
        mine = assemble(down_parts, False).reshape(-1, half_width)
        return gate_up, (mine, swap_core(mine))

    stream = tokens.astype(f32)
    saved = []
    layers = []
    parts = gather_parts(own_weights(0))
    for l in range(DECODER_LAYERS):
        att_parts, by_y, by_x, own_down = parts
        att_parts = after(att_parts, stream)
        gain_attn, gain_mlp, query_key, out_value = attention_weights(att_parts)
        normed = (normalize(stream) * gain_attn).astype(bf16)
        values = matmul(normed, out_value[:, width:]).astype(bf16)
        projected = matmul(normed, query_key)
        keys = rotary(projected[:, width:], cosine, sine).astype(bf16)
        kv = gather_pack(after(jnp.concatenate([keys, values], axis=1), by_x))
        down_parts = gather_blocks(own_down, kv)
        if l + 1 < DECODER_LAYERS:
            parts = gather_parts(after(own_weights(l + 1), kv))
        queries = rotary(projected[:, :width], cosine, sine).astype(bf16)
        queries = queries * jnp.asarray(HEAD ** (-0.5), bf16)
        mixed, logs = attend(queries, kv, key_place, bounds)
        gate_up, down = mlp_weights(*after((by_y, down_parts), mixed))
        layers.append((gain_attn, gain_mlp, query_key, out_value, gate_up, down))
        middle = stream + matmul(mixed, out_value[:, :width])
        normed_mlp = (normalize(middle) * gain_mlp).astype(bf16)
        mine = matmul(normed_mlp, gate_up[0])
        other = matmul(normed_mlp, gate_up[1])
        gate, up = pick(mine, other), pick(other, mine)
        sigmoid = jax.nn.sigmoid(gate)
        hidden = (gate * sigmoid * up).astype(bf16)
        mine = matmul(hidden, down[0])
        other = matmul(hidden, down[1])
        saved.append((stream, normed, queries, kv, logs, mixed, middle, normed_mlp, gate, up, hidden))
        stream = middle + jnp.concatenate([pick(mine, other), pick(other, mine)], axis=1)
    output = stream.astype(bf16)

    latest = done = ()
    grad = cotangent.astype(f32)
    results = [None] * DECODER_LAYERS
    for l in reversed(range(DECODER_LAYERS)):
        gain_attn, gain_mlp, query_key, out_value, gate_up, down = layers[l]
        stream, normed, queries, kv, logs, mixed, middle, normed_mlp, gate, up, hidden = saved[l]
        grad_low = grad.astype(bf16)
        grad_a, grad_b = grad_low[:, :half_width], grad_low[:, half_width:]
        grad_mine, grad_other = pick(grad_a, grad_b), pick(grad_b, grad_a)
        down_received = swap_core(cross_rows(hidden, grad_other).astype(bf16))
        down_sum = (cross_rows(hidden, grad_mine) + down_received.astype(f32)).astype(bf16)

        dhidden = matmul_nt(grad_mine, down[0]) + matmul_nt(grad_other, down[1])
        sigmoid = jax.nn.sigmoid(gate)
        dgate = (dhidden * up * sigmoid * (1.0 + gate * (1.0 - sigmoid))).astype(bf16)
        dup = (dhidden * gate * sigmoid).astype(bf16)
        dmine, dother = pick(dgate, dup), pick(dup, dgate)
        gate_up_received = swap_core(cross_rows(normed_mlp, dother).astype(bf16))
        gate_up_sum = cross_rows(normed_mlp, dmine) + gate_up_received.astype(f32)
        gate_up_sum = gate_up_sum.astype(bf16)

        dnormed = matmul_nt(dmine, gate_up[0]) + matmul_nt(dother, gate_up[1])
        dmiddle, mlp_gain_grad = normalize_back(middle, gain_mlp, dnormed)
        dmiddle = dmiddle + grad
        dmiddle_low = dmiddle.astype(bf16)
        dmixed = matmul_nt(dmiddle_low, out_value[:, :width]).astype(bf16)
        dmixed = after(dmixed, (down_sum, gate_up_sum))
        dq, dkv = attend_back(queries, kv, key_place, bounds, mixed, logs, dmixed)
        gate_up_sum = sum_over_x(after(gate_up_sum, latest))
        down_sum = sum_over_x(after(down_sum, gate_up_sum))
        dkv = after(scatter_pack(dkv), done)
        dq = rotary_back(dq, cosine, sine).astype(bf16)
        dk = rotary_back(dkv[:, :key_width], cosine, sine).astype(bf16)
        dv = dkv[:, key_width:].astype(bf16)

        dqk = jnp.concatenate([dq, dk], axis=1)
        dnormed = matmul_nt(dqk, query_key) + matmul_nt(dv, out_value[:, width:])
        dstream, attn_gain_grad = normalize_back(stream, gain_attn, dnormed)
        grad = dstream + dmiddle

        def att_terms(first):
            wide = cross_rows(
                jnp.where(first, normed, mixed), jnp.where(first, dq, dmiddle_low)
            )
            return jnp.concatenate([wide, cross_rows(normed, jnp.where(first, dk, dv))], axis=1)

        received = swap_core(att_terms(jnp.logical_not(first_core)).astype(bf16))
        att_sum = (att_terms(first_core) + received.astype(f32)).astype(bf16)
        gain_grads = jnp.stack([attn_gain_grad, mlp_gain_grad]).astype(bf16)
        received = swap_core(gain_grads)
        gain_grads = (gain_grads.astype(f32) + received.astype(f32)).astype(bf16)
        gain_grads = gain_grads.reshape(2, -1, shard).swapaxes(0, 1)
        gain_grads = jnp.pad(gain_grads, ((0, 0), (0, 6), (0, att_width - shard)))
        att_sum = jnp.concatenate([att_sum.reshape(-1, shard, att_width), gain_grads], axis=1)
        att_sum = sum_over_x(after(att_sum.reshape(-1, att_width), down_sum))
        latest = att_sum

        att_pair = att_sum.reshape(2, shard + 8, att_width)
        down_pair = down_sum.reshape(2, -1, half_width)
        gate_up_pair = gate_up_sum.reshape(2, shard, -1)
        if l > 0:
            done = finish_sums([att_pair, down_pair, gate_up_pair])
            (att_own, down_own, gate_up_own), (att_other, down_other, gate_up_other) = done
        else:
            mlp = finish_sums([down_pair, gate_up_pair])
            (down_own, gate_up_own), (down_other, gate_up_other) = mlp
            (att_own,), (att_other,) = finish_sums([att_pair])
        att_a, att_b = pick(att_own, att_other), pick(att_other, att_own)
        results[l] = (
            att_own[shard, :shard],
            att_a[:shard, :width],
            att_a[:shard, width:],
            att_b[:shard, width:],
            att_b[:shard, :width],
            att_own[shard + 1, :shard],
            pick(gate_up_own, gate_up_other),
            pick(gate_up_other, gate_up_own),
            jnp.concatenate([pick(down_own, down_other), pick(down_other, down_own)], axis=1),
        )
    stacked = [
        jnp.stack([results[l][m].astype(f32) for l in range(DECODER_LAYERS)], axis=0)
        for m in range(9)
    ]
    return (output, grad, *stacked)


def solution(mesh):
    weights = P(None, "fsdp", None)
    gains = P(None, "fsdp")
    packed = P(("rep", "fsdp"), None)
    in_specs = (
        packed,
        P("rep", None),
        gains,
        weights,
        weights,
        weights,
        weights,
        gains,
        weights,
        weights,
        weights,
        packed,
    )
    out_specs = (
        packed,
        packed,
        gains,
        weights,
        weights,
        weights,
        weights,
        gains,
        weights,
        weights,
        weights,
    )
    return jax.shard_map(body, mesh=mesh, in_specs=in_specs, out_specs=out_specs, check_vma=False)
```
